32 devices in a mesh: dp: 4 (over z), fsdp: 8 (over y, x, core).
Axes of the slice: x: 2, y: 2, z: 4, core: 2. Of those that a mesh axis runs over, the one named last changes fastest.
Arguments:
- tokens_in: bfloat16 [32768, 768], P(('dp', 'fsdp')), may hold values from -6 to 6
- w_qkv: bfloat16 [768, 2304], P(('dp', 'fsdp')), may hold values from -0.21875 to 0.21875
- w_attn_out: bfloat16 [768, 768], P(('dp', 'fsdp')), may hold values from -1.75 to 1.75
- gain_attn: bfloat16 [768], P(('dp', 'fsdp')), may hold values from 0.5 to 1.5
- gain_ffn: bfloat16 [768], P(('dp', 'fsdp')), may hold values from 0.5 to 1.5
- rel_bias: bfloat16 [768], P(('dp', 'fsdp')), may hold values from -3 to 3
- router: bfloat16 [768, 4], P(('dp', 'fsdp')), may hold values from -0.15625 to 0.15625
- w_in: bfloat16 [768, 12288], P('dp', 'fsdp'), may hold values from -0.21875 to 0.21875
- w_out: bfloat16 [768, 12288], P('dp', 'fsdp'), may hold values from -0.15625 to 0.15625
- segment_ids: int32 [32, 1024], P(('dp', 'fsdp')), may hold values from 0 to 3, never falling along the last dimension, each value on 1 to 512 neighbouring positions
- expert_ids: int32 [32768, 2], P(('dp', 'fsdp')), may hold values from 0 to 3, all different within a row; in each aligned block of 1024 rows (0 to 1023, 1024 to 2047, ...) at most 640 rows name the same one
- d_out: bfloat16 [32768, 768], P(('dp', 'fsdp')), may hold values from -6 to 6
Outputs:
- out: bfloat16 [32768, 768], P(('dp', 'fsdp'))
- d_tokens: float32 [32768, 768], P(('dp', 'fsdp'))
- d_w_qkv: float32 [768, 2304], P(('dp', 'fsdp'))
- d_w_attn_out: float32 [768, 768], P(('dp', 'fsdp'))
- d_gain_attn: float32 [768], P(('dp', 'fsdp'))
- d_gain_ffn: float32 [768], P(('dp', 'fsdp'))
- d_rel_bias: float32 [768], P(('dp', 'fsdp'))
- d_router: float32 [768, 4], P(('dp', 'fsdp'))
- d_w_in: float32 [768, 12288], P('dp', 'fsdp')
- d_w_out: float32 [768, 12288], P('dp', 'fsdp')
The draws below stay inside these ranges and needn't reach their ends.
Inputs may be any that keep to these rules, and one draw needn't show every extreme that they name: `segment_ids`: along a sequence the numbers never fall; each document has 1 to 512 positions, and one has exactly 512. `expert_ids`: each row names 2 different experts. Among the rows of one device (aligned blocks of 1024 rows), no expert is named more than 640 times, a bound that some block reaches.
All inputs are finite; a program needn't handle non-finite values.
Results may differ from the reference program's by a relative error of at most 0.014.
Values may be sent and summed in bfloat16 or wider, within the bound.
No kernel may reach another device: no remote copies, remote signals or barrier semaphores. Data moves between devices by JAX's collectives and lax.ppermute only.
A program may use at most 704 MiB of HBM per device.

```python
import math
import jax
import jax.numpy as jnp
import numpy as np
from jax import lax

D = 768
HEADS = 12
HEAD_DIM = 64
FF = 3072
TOP = 2
BUCKETS = 64
MAX_DIST = 128
LEN = 1024
EXPERTS = 4
TOK_DEV = 1024
SEQS = 32
TOKENS = 32768
CAP = 640


def block_scale(stream_key, dims, pieces, smallest, top_value):
    gain = 1.0
    for position, blocks in pieces:
        heights = jax.random.uniform(jax.random.fold_in(jax.random.fold_in(stream_key, 6), position), (blocks,), jnp.float32, smallest / len(pieces), top_value / len(pieces))
        gain = gain * jnp.repeat(jnp.exp(heights), dims[position] // blocks).reshape((-1,) + (1,) * (len(dims) - 1 - position))
    return gain


def length_profile(count, total, reach, skew):
    loads = [(1 << 20) // math.isqrt(grade ** skew) + 1 for grade in range(2, count + 1)]
    surplus, holding = total - reach - (count - 1), [1] * (count - 1)
    while surplus > 0:
        candidates = [i for i in range(count - 1) if holding[i] < reach]
        pool, remaining = sum([loads[i] for i in candidates]), surplus
        for i in candidates:
            more = min(reach - holding[i], max(1, remaining * loads[i] // pool), surplus)
            holding[i] = holding[i] + more
            surplus = surplus - more
    return np.array([reach] + holding)


def ragged_sizes(stream_key, count, total, limit, slope):
    if count == 2:
        one = jax.random.randint(stream_key, (), max(1, total - limit), min(limit, total - 1) + 1)
        return jnp.stack([one, total - one])
    tallies = jnp.asarray(length_profile(count, total, limit, slope), jnp.int32)
    pairs = (count - 1) // 2
    donor, sink = tallies[1:1 + 2 * pairs:2], tallies[2:2 + 2 * pairs:2]
    room = jnp.minimum(donor - 1, limit - sink)
    passed = jax.random.randint(jax.random.fold_in(stream_key, 1), (pairs,), 0, 1 << 20) % (room + 1)
    tallies = tallies.at[1:1 + 2 * pairs:2].set(donor - passed).at[2:2 + 2 * pairs:2].set(sink + passed)
    return tallies[jax.random.permutation(jax.random.fold_in(stream_key, 2), count)]


def shared_out(rng, own, number, rows, number_of, top, bound, skew):
    ranking = jax.random.permutation(rng, number_of)
    packed, ordinary = shares(number_of, rows * top, bound, skew, True), shares(number_of, rows * top, bound, skew, False)
    places = jnp.arange(number_of)

    def named(lengths, rotation):
        used = int((lengths > 0).sum())
        fixed = max(1, used // 4)
        shifted = fixed + (places - fixed + rotation * (used - fixed)) % max(1, number_of - fixed)
        return jnp.zeros((number_of,), jnp.int32).at[ranking[jnp.where(places < fixed, places, shifted)]].set(jnp.asarray(lengths, jnp.int32))

    lengths = jnp.where(number % 4 == 0, named(packed, number // 4), named(ordinary, number - number // 4 - 1))
    mixed = jax.random.permutation(jax.random.fold_in(own, 3), number_of)
    giver, sink = mixed[0:number_of // 2 * 2:2], mixed[1:number_of // 2 * 2:2]
    slack = jnp.minimum(lengths[giver] - 1, bound - lengths[sink]) // 2
    slack = jnp.where((giver == ranking[0]) | (sink == ranking[0]) | (lengths[sink] == 0), 0, jnp.maximum(slack, 0))
    shifted = jax.random.randint(jax.random.fold_in(own, 4), (number_of // 2,), 0, 1 << 20) % (slack + 1)
    lengths = lengths.at[giver].add(-shifted).at[sink].add(shifted)
    items = jnp.searchsorted(jnp.cumsum(lengths), jnp.arange(rows * top), side="right").astype(jnp.int32)
    table = items.reshape(top, rows).T
    table = table[jax.random.permutation(jax.random.fold_in(own, 1), rows)]
    rotation = jax.random.randint(jax.random.fold_in(own, 2), (rows, 1), 0, top)
    return jnp.take_along_axis(table, (jnp.arange(top)[None, :] + rotation) % top, axis=1)


def shares(amount, total, reach, skew, full):
    loads = [(1 << 20) // math.isqrt(rank ** skew) + 1 for rank in range(1, amount + 1)]
    largest = reach if full else min(reach, max(-(-total // amount), total * loads[0] // sum(loads)))
    least = 1 if total - largest >= amount - 1 else 0
    holding, rest = [largest] + [least] * (amount - 1), total - largest - least * (amount - 1)
    while rest > 0:
        candidates = [i for i in range(1, amount) if holding[i] < largest] or [i for i in range(1, amount) if holding[i] < reach]
        mass, budget = sum([loads[i] for i in candidates]), rest
        for i in candidates:
            addition = min(reach - holding[i], max(1, budget * loads[i] // mass), rest)
            holding[i] = holding[i] + addition
            rest = rest - addition
    return np.array(holding)


def gaussian(key, dims, width, most, shards=(), kind=jnp.bfloat16):
    values = jax.random.normal(key, dims, jnp.float32) * width
    if len(shards) > 0:
        values = block_scale(key, dims, shards, -0.22, 0.18) * values
    return jnp.clip(values, min=-most, max=most).astype(kind)


def setup_inputs(seed: int = 0) -> dict:
    key_list = jax.random.split(jax.random.key(seed), 13)
    tokens_in = gaussian(key_list[0], (TOKENS, D), 1.0, 6.0, ((0, 32),))
    w_qkv = gaussian(key_list[1], (D, 3 * D), D ** -0.5, 0.21875, ((0, 32),))
    w_attn_out = gaussian(key_list[2], (D, D), (D // 64) ** -0.5, 1.75, ((0, 32),))
    gain_attn = jnp.clip(1.0 + 0.1 * jax.random.normal(key_list[3], (D,), jnp.float32), 0.5, 1.5).astype(jnp.bfloat16)
    gain_ffn = jnp.clip(1.0 + 0.1 * jax.random.normal(key_list[4], (D,), jnp.float32), 0.5, 1.5).astype(jnp.bfloat16)
    rel_bias = gaussian(key_list[5], (HEADS * BUCKETS,), 1.0, 3.0, ((0, 32),))
    router = gaussian(key_list[6], (D, EXPERTS), (2 * D) ** -0.5, 0.15625, ((0, 32),))
    w_in = gaussian(key_list[7], (D, EXPERTS * FF), D ** -0.5, 0.21875, ((0, 4), (1, 8)))
    w_out = gaussian(key_list[8], (D, EXPERTS * FF), (FF // 2) ** -0.5, 0.15625, ((0, 4), (1, 8)))
    segment_ids = jax.vmap(lambda own: jnp.searchsorted(jnp.cumsum(ragged_sizes(own, max(3, LEN // 256), LEN, LEN // 2, 1)), jnp.arange(LEN), side="right"))(jax.random.split(key_list[9], SEQS)).reshape((SEQS, LEN)).astype(jnp.int32)
    expert_ids_keys = jax.random.split(jax.random.fold_in(key_list[10], 1), TOKENS // TOK_DEV)
    expert_ids_turns = jax.random.permutation(jax.random.fold_in(key_list[10], 3), TOKENS // TOK_DEV)
    expert_ids = jax.vmap(lambda own, number: shared_out(jax.random.fold_in(key_list[10], 2), own, number, TOK_DEV, EXPERTS, TOP, CAP, 0))(expert_ids_keys, expert_ids_turns).reshape((TOKENS, TOP))
    d_out = gaussian(key_list[11], (TOKENS, D), 1.0, 6.0, ((0, 32),))
    return dict(tokens_in=tokens_in, w_qkv=w_qkv, w_attn_out=w_attn_out, gain_attn=gain_attn, gain_ffn=gain_ffn, rel_bias=rel_bias, router=router, w_in=w_in, w_out=w_out, segment_ids=segment_ids, expert_ids=expert_ids, d_out=d_out)


@jax.custom_vjp
def low(v):
    return lax.optimization_barrier(v.astype(jnp.bfloat16)).astype(jnp.float32)

@jax.custom_vjp
def low_back(v):
    return v

def low_keep(v):
    return (low(v), None)

def low_pass(kept, grad):
    return (grad,)

def back_keep(v):
    return (v, None)

def back_low(kept, grad):
    return (low(grad),)
low.defvjp(low_keep, low_pass)
low_back.defvjp(back_keep, back_low)
EPS = 1e-06
NEG = -1e+30
PRECISE = lax.Precision.HIGHEST

def bucket_bounds(bucket_count, max_distance):
    halfway = bucket_count // 2
    bounds = []
    for bucket in range(bucket_count):
        if bucket < halfway:
            bounds.append(bucket)
        else:
            bounds.append(int(math.ceil(halfway * (max_distance / halfway) ** ((bucket - halfway) / halfway))))
    return bounds

def distance_buckets(length):
    limits = jnp.array(bucket_bounds(BUCKETS, MAX_DIST), dtype=jnp.int32)
    distance = jnp.arange(length, dtype=jnp.int32)
    reached = (distance[:, None] >= limits[None, :]).astype(jnp.int32)
    return (lax.optimization_barrier(jnp.sum(reached, axis=1)) - 1).astype(jnp.int32)

def rms_norm(values, gain_vec):
    return values * lax.rsqrt(lax.optimization_barrier(jnp.mean(values * values, axis=-1, keepdims=True)) + EPS) * gain_vec

def reference(tokens_in, w_qkv, w_attn_out, gain_attn, gain_ffn, rel_bias, router, w_in, w_out, segment_ids, expert_ids, d_out):
    block_count = TOKENS // TOK_DEV
    assigned = TOK_DEV * TOP
    half_ff = FF // 2
    flat_ids = expert_ids.reshape(block_count, assigned).astype(jnp.int32)
    expert_hot = (flat_ids[:, :, None] == jnp.arange(EXPERTS, dtype=jnp.int32)[None, None, :]).astype(jnp.int32)
    earlier = (jnp.cumsum(expert_hot, axis=1) - 1).astype(jnp.int32)
    slot_of = lax.optimization_barrier(jnp.sum(expert_hot * earlier, axis=2)).astype(jnp.int32)
    block_of = jnp.broadcast_to(jnp.arange(block_count, dtype=jnp.int32)[:, None], flat_ids.shape)
    token_of = (block_of * TOK_DEV + jnp.arange(assigned, dtype=jnp.int32)[None, :] // TOP).astype(jnp.int32)
    slot_table = jnp.full((EXPERTS, block_count, CAP), TOKENS, jnp.int32).at[flat_ids, block_of, slot_of].set(token_of)
    slot_table = slot_table.reshape(EXPERTS, block_count * CAP)
    pick_index = ((flat_ids * block_count + block_of) * CAP + slot_of).reshape(-1).astype(jnp.int32)
    bucket_ids = distance_buckets(LEN)
    distance = jnp.arange(LEN, dtype=jnp.int32)
    rel_dist = jnp.maximum(distance[:, None] - distance[None, :], 0).astype(jnp.int32)
    causal = distance[:, None] >= distance[None, :]
    scaling = HEAD_DIM ** (-0.5)

    def forward(tokens_f, wqkv_f, wattn_f, gain_a, gain_f, bias_flat, router_f, w_first, w_second):
        normed_attn = low(rms_norm(tokens_f, gain_a))
        qkv_rows = low(low_back(jnp.dot(normed_attn, wqkv_f, precision=PRECISE)))
        qkv_parts = qkv_rows.reshape(SEQS, LEN, 3, HEADS, HEAD_DIM)
        bias_rel = jnp.take(bias_flat.reshape(HEADS, BUCKETS), bucket_ids, axis=1)
        bias_full = jnp.take(bias_rel, rel_dist, axis=1)

        def attend(pair):
            sequence, segments = pair
            query_rows = sequence[:, 0]
            key_rows = sequence[:, 1]
            value_rows = sequence[:, 2]
            raw_scores = jnp.einsum('qhd,khd->hqk', query_rows, key_rows, precision=PRECISE) * scaling + bias_full
            allowed = causal & (segments[:, None] == segments[None, :])
            raw_scores = low_back(jnp.where(allowed[None], raw_scores, NEG))
            probs_low = low(jax.nn.softmax(raw_scores, axis=-1))
            mixed_out = jnp.einsum('hqk,khd->qhd', probs_low, value_rows, precision=PRECISE)
            return low(low_back(mixed_out)).reshape(LEN, D)
        mixed_rows = lax.map(jax.checkpoint(attend), (qkv_parts, segment_ids)).reshape(TOKENS, D)
        branch = low_back(jnp.dot(mixed_rows, wattn_f, precision=PRECISE))
        residual = tokens_f + branch
        normed_ffn = low(rms_norm(residual, gain_f))
        logits = jnp.dot(normed_ffn, router_f, precision=PRECISE)
        gates_soft = jax.nn.softmax(jnp.take_along_axis(logits, expert_ids, axis=1), axis=1)
        padded = jnp.concatenate([normed_ffn, jnp.zeros((1, D), jnp.float32)], axis=0)

        def expert(triple):
            first_w, second_w, row_index = triple
            total = jnp.zeros((row_index.shape[0], D), jnp.float32)
            for half in range(2):
                columns = slice(half * half_ff, (half + 1) * half_ff)
                rows_in = low_back(padded[row_index])
                pre_act = low_back(jnp.dot(rows_in, first_w[:, columns], precision=PRECISE))
                hidden = low(jax.nn.gelu(pre_act, approximate=True))
                partial_out = low(low_back(jnp.dot(hidden, second_w[:, columns].T, precision=PRECISE)))
                total = total + partial_out
            return total
        first_all = jnp.transpose(w_first.reshape(D, EXPERTS, FF), (1, 0, 2))
        second_all = jnp.transpose(w_second.reshape(D, EXPERTS, FF), (1, 0, 2))
        expert_outs = lax.map(jax.checkpoint(expert), (first_all, second_all, slot_table))
        picked = expert_outs.reshape(EXPERTS * block_count * CAP, D)[pick_index].reshape(TOKENS, TOP, D)
        return residual + lax.optimization_barrier(jnp.sum(gates_soft[:, :, None] * picked, axis=1))
    primals = (tokens_in.astype(jnp.float32), w_qkv.astype(jnp.float32), w_attn_out.astype(jnp.float32), gain_attn.astype(jnp.float32), gain_ffn.astype(jnp.float32), rel_bias.astype(jnp.float32), router.astype(jnp.float32), w_in.astype(jnp.float32), w_out.astype(jnp.float32))
    result, pull_back = jax.vjp(forward, *primals)
    grads = pull_back(d_out.astype(jnp.float32))
    return (result.astype(jnp.bfloat16), grads[0], grads[1], grads[2], grads[3], grads[4], grads[5], grads[6], grads[7], grads[8])
```

```python
import functools
import math

import jax
import jax.numpy as jnp
from jax import lax
from jax.experimental import pallas as pl
from jax.experimental.pallas import tpu as pltpu
from jax.sharding import PartitionSpec as P

NEG = -1e30
BLK = 256
SPAN = 2
F32 = jnp.float32
BF16 = jnp.bfloat16
LIGHT = pl.CostEstimate(flops=1000, bytes_accessed=1000, transcendentals=0)


def dot_nt(a, b):
    return lax.dot_general(a, b, (((1,), (1,)), ((), ())), preferred_element_type=F32)


def dot_nn(a, b):
    return lax.dot_general(a, b, (((1,), (0,)), ((), ())), preferred_element_type=F32)


def fill_masks(mask, seg_row, seg_col, blocks):
    key_place = lax.broadcasted_iota(jnp.int32, (BLK, BLK), 0)
    row_place = lax.broadcasted_iota(jnp.int32, (BLK, BLK), 1)
    for kb in range(blocks):
        keys = seg_col[kb * BLK : (kb + 1) * BLK, :]
        for step in range(min(SPAN + 1, blocks - kb)):
            rows = seg_row[:, (kb + step) * BLK : (kb + step + 1) * BLK]
            seen = keys == rows
            if step == 0:
                seen = seen & (row_place >= key_place)
            mask[kb, step] = jnp.where(seen, 0.0, NEG)


def bias_tiles(near_row, far_value):
    key_place = lax.broadcasted_iota(jnp.int32, (BLK, BLK), 0)
    row_place = lax.broadcasted_iota(jnp.int32, (BLK, BLK), 1)
    rolled = pltpu.roll(
        jnp.broadcast_to(near_row, (BLK, BLK)), 0, 1, stride=1, stride_axis=0
    )
    return rolled, jnp.where(row_place < key_place, rolled, far_value)


def head_lanes(values, half):
    lane = lax.broadcasted_iota(jnp.int32, values.shape, 1)
    keep = (lane >= 64) if half else (lane < 64)
    return jnp.where(keep, values, jnp.zeros_like(values))


def attn_fwd_kernel(
    far_ref, q_ref, k_ref, v_ref, near_ref, seg_row, seg_col, *rest
):
    o_ref, lse_ref, mask, turned = rest[-4:]
    pair = pl.program_id(0)
    length = q_ref.shape[0]
    blocks = length // BLK

    @pl.when(pair == 0)
    def _():
        fill_masks(mask, seg_row, seg_col, blocks)

    v_turned = v_ref[...].T
    ones = jnp.ones((16, length), BF16)
    for half in range(2):
        far_value = far_ref[pair * 2 + half]
        diag, below = bias_tiles(near_ref[0, half : half + 1, :], far_value)
        keys = head_lanes(k_ref[...], half)
        values = jnp.concatenate([v_turned[64 * half : 64 * half + 64], ones], axis=0)
        for a in range(blocks):
            first = max(0, a - SPAN)
            q_rows = q_ref[a * BLK : (a + 1) * BLK, :] * jnp.asarray(0.125, BF16)
            parts = []
            for kb in range(first, a + 1):
                part = dot_nt(keys[kb * BLK : (kb + 1) * BLK], q_rows)
                bias = (diag, below, far_value)[a - kb]
                parts.append(part + bias + mask[kb, a - kb])
            peak = functools.reduce(
                jnp.maximum, [jnp.max(part, axis=0, keepdims=True) for part in parts]
            )
            weights = jnp.concatenate(
                [jnp.exp(part - peak).astype(BF16) for part in parts], axis=0
            )
            made = dot_nn(values[:, first * BLK : (a + 1) * BLK], weights)
            total = made[64:65]
            turned[64 * half : 64 * half + 64, a * BLK : (a + 1) * BLK] = made[:64] / total
            lse_ref[0, half : half + 1, a * BLK : (a + 1) * BLK] = peak + jnp.log(total)
    o_ref[...] = turned[...].T.astype(BF16)


def attn_bwd_kernel(
    far_ref, q_ref, k_ref, v_ref, g_ref, o_ref, lse_ref, near_ref, seg_row, seg_col, *rest
):
    d_ref, near_grad, far_grad, mask, turned = rest[-5:]
    pair = pl.program_id(0)
    length = q_ref.shape[0]
    blocks = length // BLK

    @pl.when(pair == 0)
    def _():
        fill_masks(mask, seg_row, seg_col, blocks)

    scaled = q_ref[...] * jnp.asarray(0.125, BF16)
    k_turned = k_ref[...].T
    ones = jnp.ones((16, length), BF16)
    inner = (g_ref[...].astype(F32) * o_ref[...].astype(F32)).T
    key_place = lax.broadcasted_iota(jnp.int32, (BLK, BLK), 0)
    row_place = lax.broadcasted_iota(jnp.int32, (BLK, BLK), 1)
    key_grads = [None] * blocks
    value_grads = [None] * blocks
    for half in range(2):
        far_value = far_ref[pair * 2 + half]
        diag, below = bias_tiles(near_ref[0, half : half + 1, :], far_value)
        keys = head_lanes(k_ref[...], half)
        values = head_lanes(v_ref[...], half)
        q_own = head_lanes(scaled, half)
        g_own = head_lanes(g_ref[...], half)
        keys_turned = jnp.concatenate([k_turned[64 * half : 64 * half + 64], ones], axis=0)
        delta = jnp.sum(inner[64 * half : 64 * half + 64], axis=0, keepdims=True)
        lse = lse_ref[0, half : half + 1, :]
        diag_grad = jnp.zeros((BLK, BLK), F32)
        below_grad = jnp.zeros((BLK, BLK), F32)
        turned[...] = jnp.zeros_like(turned)
        for kb in range(blocks):
            last = min(kb + SPAN + 1, blocks)
            k_rows = keys[kb * BLK : (kb + 1) * BLK]
            v_rows = values[kb * BLK : (kb + 1) * BLK]
            probs, grads = [], []
            for a in range(kb, last):
                rows = slice(a * BLK, (a + 1) * BLK)
                score = dot_nt(k_rows, scaled[rows])
                d_prob = dot_nt(v_rows, g_ref[rows, :])
                bias = (diag, below, far_value)[a - kb]
                prob = jnp.exp(score + bias + mask[kb, a - kb] - lse[:, rows])
                d_score = prob * (d_prob - delta[:, rows])
                if a == kb:
                    diag_grad = diag_grad + d_score
                elif a == kb + 1:
                    below_grad = below_grad + d_score
                probs.append(prob.astype(BF16))
                grads.append(d_score.astype(BF16))
            wide = slice(kb * BLK, last * BLK)
            prob_wide = jnp.concatenate(probs, axis=1)
            grad_wide = jnp.concatenate(grads, axis=1)
            value_grad = dot_nn(prob_wide, g_own[wide])
            key_grad = dot_nn(grad_wide, q_own[wide])
            turned[:, wide] += dot_nn(keys_turned[:, kb * BLK : (kb + 1) * BLK], grad_wide)
            if half == 0:
                value_grads[kb], key_grads[kb] = value_grad, key_grad
            else:
                rows = slice(kb * BLK, (kb + 1) * BLK)
                d_ref[2, rows, :] = (value_grads[kb] + value_grad).astype(BF16)
                d_ref[1, rows, :] = (key_grads[kb] + key_grad).astype(BF16)
        part = (turned[:64] * 0.125).T
        if half == 0:
            first_part = part
        else:
            d_ref[0] = jnp.concatenate([first_part, part], axis=1).astype(BF16)
        by_offset = diag_grad + jnp.where(row_place < key_place, below_grad, 0.0)
        for bit in range(8):
            by_offset = jnp.where(
                ((key_place >> bit) & 1) == 1,
                pltpu.roll(by_offset, BLK - (1 << bit), 1),
                by_offset,
            )
        near = jnp.sum(by_offset, axis=0, keepdims=True)
        near_grad[0, half : half + 1, :] = near
        everything = jnp.sum(turned[64:65, :], axis=1, keepdims=True)
        rest = everything - jnp.sum(near, axis=1, keepdims=True)
        far_grad[0, half : half + 1, :] = jnp.broadcast_to(rest, (1, 128))


def attention_specs(length, pairs):
    def column(offset):
        return pl.BlockSpec((length, 128), lambda p, far: (0, p + offset))

    return column


def attention_forward(qkv_rows, segments, near, far, heads, ahead=()):
    length = qkv_rows.shape[0]
    pairs = heads // 2
    width = heads * 64
    column = attention_specs(length, pairs)
    blocks = length // BLK
    return pl.pallas_call(
        attn_fwd_kernel,
        grid_spec=pltpu.PrefetchScalarGridSpec(
            num_scalar_prefetch=1,
            grid=(pairs,),
            in_specs=[
                column(0),
                column(pairs),
                column(2 * pairs),
                pl.BlockSpec((1, 2, BLK), lambda p, far: (p, 0, 0)),
                pl.BlockSpec((1, length), lambda p, far: (0, 0)),
                pl.BlockSpec((length, 1), lambda p, far: (0, 0)),
            ]
            + [pl.BlockSpec(memory_space=pl.ANY)] * len(ahead),
            out_specs=[
                column(0),
                pl.BlockSpec((1, 2, length), lambda p, far: (p, 0, 0)),
            ],
            scratch_shapes=[
                pltpu.VMEM((blocks, SPAN + 1, BLK, BLK), F32),
                pltpu.VMEM((128, length), F32),
            ],
        ),
        out_shape=[
            jax.ShapeDtypeStruct((length, width), BF16),
            jax.ShapeDtypeStruct((pairs, 2, length), F32),
        ],
        compiler_params=pltpu.CompilerParams(vmem_limit_bytes=60 * 1024 * 1024),
        cost_estimate=LIGHT,
        name="attention_forward",
    )(far, qkv_rows, qkv_rows, qkv_rows, near, segments.reshape(1, length), segments.reshape(length, 1), *ahead)


def attention_backward(qkv_rows, d_mixed, mixed, lse, segments, near, far, heads, ahead=()):
    length = qkv_rows.shape[0]
    pairs = heads // 2
    width = heads * 64
    column = attention_specs(length, pairs)
    blocks = length // BLK
    small = lambda n: pl.BlockSpec((1, 2, n), lambda p, far: (p, 0, 0))
    return pl.pallas_call(
        attn_bwd_kernel,
        grid_spec=pltpu.PrefetchScalarGridSpec(
            num_scalar_prefetch=1,
            grid=(pairs,),
            in_specs=[
                column(0),
                column(pairs),
                column(2 * pairs),
                column(0),
                column(0),
                small(length),
                small(BLK),
                pl.BlockSpec((1, length), lambda p, far: (0, 0)),
                pl.BlockSpec((length, 1), lambda p, far: (0, 0)),
            ]
            + [pl.BlockSpec(memory_space=pl.ANY)] * len(ahead),
            out_specs=[
                pl.BlockSpec((3, length, 128), lambda p, far: (0, 0, p)),
                small(BLK),
                small(128),
            ],
            scratch_shapes=[
                pltpu.VMEM((blocks, SPAN + 1, BLK, BLK), F32),
                pltpu.VMEM((80, length), F32),
            ],
        ),
        out_shape=[
            jax.ShapeDtypeStruct((3, length, width), BF16),
            jax.ShapeDtypeStruct((pairs, 2, BLK), F32),
            jax.ShapeDtypeStruct((pairs, 2, 128), F32),
        ],
        compiler_params=pltpu.CompilerParams(vmem_limit_bytes=60 * 1024 * 1024),
        cost_estimate=LIGHT,
        name="attention_backward",
    )(
        far, qkv_rows, qkv_rows, qkv_rows, d_mixed, mixed, lse, near,
        segments.reshape(1, length), segments.reshape(length, 1), *ahead,
    )


HEADS = 12
BUCKETS = 64
MAX_DIST = 128
EPS = 1e-06
ROWS = 256
TAIL = 16
COEF = math.sqrt(2.0 / math.pi)
CUBIC = 0.044715
MIB = 1024 * 1024


def bucket_bounds(bucket_count, max_distance):
    halfway = bucket_count // 2
    bounds = []
    for bucket in range(bucket_count):
        if bucket < halfway:
            bounds.append(bucket)
        else:
            bounds.append(
                int(math.ceil(halfway * (max_distance / halfway) ** ((bucket - halfway) / halfway)))
            )
    return bounds


def buckets_of(distance):
    limits = jnp.array(bucket_bounds(BUCKETS, MAX_DIST), dtype=jnp.int32)
    reached = (distance[:, None] >= limits[None, :]).astype(jnp.int32)
    return jnp.sum(reached, axis=1) - 1


def whole(shape):
    return pl.BlockSpec(shape, lambda *_: (0,) * len(shape))


def split_three(values):
    high = values.astype(BF16)
    rest = values - high.astype(F32)
    middle = rest.astype(BF16)
    low = (rest - middle.astype(F32)).astype(BF16)
    return high, middle, low


ANY = pl.BlockSpec(memory_space=pl.ANY)


def dispatch_kernel(experts, dest_ref, values_ref, gate_ref, *rest):
    out_refs = rest[-experts:]
    slots = out_refs[0].shape[0] - TAIL
    tokens = values_ref.shape[0]
    place = lax.broadcasted_iota(jnp.int32, (slots, tokens), 0)
    hot = (place == dest_ref[0]).astype(F32).astype(BF16)
    rows = dot_nn(hot, values_ref[...]).astype(BF16)
    pieces = split_three(jnp.broadcast_to(gate_ref[0], (TAIL, tokens)))
    line = lax.broadcasted_iota(jnp.int32, (TAIL, tokens), 0)
    stacked = jnp.zeros((TAIL, tokens), F32)
    for index, piece in enumerate(pieces):
        stacked = jnp.where(line == index, piece.astype(F32), stacked)
    tail = dot_nt(stacked.astype(BF16), hot).astype(BF16)
    for index, out_ref in enumerate(out_refs):

        @pl.when(pl.program_id(0) == index)
        def _():
            out_ref[:slots, :] = rows
            out_ref[slots:, :] = jnp.zeros((TAIL, out_ref.shape[1]), BF16)
            out_ref[slots:, :slots] = tail


def dispatch(dest_row, values, gate_row, slots, ahead=()):
    experts = dest_row.shape[0]
    tokens, width = values.shape
    return pl.pallas_call(
        functools.partial(dispatch_kernel, experts),
        grid=(experts,),
        in_specs=[
            pl.BlockSpec((1, 1, tokens), lambda m: (m, 0, 0)),
            whole((tokens, width)),
            pl.BlockSpec((1, 1, tokens), lambda m: (m, 0, 0)),
        ]
        + [ANY] * len(ahead),
        out_specs=[whole((slots + TAIL, width))] * experts,
        out_shape=[jax.ShapeDtypeStruct((slots + TAIL, width), BF16)] * experts,
        compiler_params=pltpu.CompilerParams(vmem_limit_bytes=40 * MIB),
        cost_estimate=LIGHT,
        name="dispatch_rows",
    )(dest_row, values, gate_row, *ahead)


def nothing_kernel(*refs):
    pass


def held(values, ahead):
    count = len(values)
    return pl.pallas_call(
        nothing_kernel,
        in_specs=[ANY] * (count + len(ahead)),
        out_specs=[ANY] * count,
        out_shape=[jax.ShapeDtypeStruct(value.shape, value.dtype) for value in values],
        input_output_aliases={index: index for index in range(count)},
        cost_estimate=LIGHT,
        name="held",
    )(*values, *ahead)


def post_kernel(
    mixed_ref, w_ref, tokens_ref, gain_ref, router_ref, dest_ref, move_ref, *rest
):
    residual_ref, normed_ref, gates_ref, moved_ref = rest[-4:]
    moved = dot_nn(mixed_ref[...], move_ref[...]).astype(BF16)
    moved_ref[...] = moved
    residual = tokens_ref[...].astype(F32) + dot_nn(moved, w_ref[...])
    residual_ref[...] = residual
    scale = lax.rsqrt(jnp.mean(residual * residual, axis=1, keepdims=True) + EPS)
    normed = (residual * scale * gain_ref[...]).astype(BF16)
    normed_ref[...] = normed
    logits = dot_nn(normed, router_ref[...])
    chosen = dest_ref[...] >= 0
    logits = jnp.where(chosen, logits, NEG)
    peak = jnp.max(logits, axis=1, keepdims=True)
    weights = jnp.where(chosen, jnp.exp(logits - peak), 0.0)
    gates_ref[...] = weights / jnp.sum(weights, axis=1, keepdims=True)


def post_attention(mixed, w_out, tokens, gain, router, dest_col, move, ahead=()):
    rows, width = tokens.shape
    block = lambda n: pl.BlockSpec((ROWS, n), lambda i: (i, 0))
    return pl.pallas_call(
        post_kernel,
        grid=(rows // ROWS,),
        in_specs=[
            block(width), pl.BlockSpec((width, width), lambda i: (0, 3)), block(width),
            whole((1, width)), whole((width, 128)), block(128), whole((width, width)),
        ]
        + [ANY] * len(ahead),
        out_specs=[block(width), block(width), block(128), block(width)],
        out_shape=[
            jax.ShapeDtypeStruct((rows, width), F32),
            jax.ShapeDtypeStruct((rows, width), BF16),
            jax.ShapeDtypeStruct((rows, 128), F32),
            jax.ShapeDtypeStruct((rows, width), BF16),
        ],
        compiler_params=pltpu.CompilerParams(vmem_limit_bytes=32 * MIB),
        cost_estimate=LIGHT,
        name="post_attention",
    )(mixed, w_out, tokens, gain, router, dest_col, move, *ahead)


def expert_kernel(
    rows_ref, grads_ref, in_own, out_own, in_other, out_other, *rest
):
    hid_own, hid_other, dpre_own, dpre_other, back_ref, made_ref = rest[-11:-5]
    rows_turned, gexp_turned, gexp, made_sum, back_sum = rest[-5:]
    step = pl.program_id(0)
    slots = gexp.shape[0]

    @pl.when(step == 0)
    def _():
        turned = rows_ref[slots:, :slots].astype(F32).T
        gate = jnp.sum(turned, axis=1, keepdims=True)
        gexp[...] = (grads_ref[:slots, :].astype(F32) * gate).astype(BF16)
        gexp_turned[...] = gexp[...].T
        rows_turned[...] = rows_ref[:slots, :].T
        made_sum[...] = jnp.zeros_like(made_sum)
        back_sum[...] = jnp.zeros_like(back_sum)

    rows = rows_ref[:slots, :]
    for w_in, w_out, hid, dpre in (
        (in_own, out_own, hid_own, dpre_own),
        (in_other, out_other, hid_other, dpre_other),
    ):
        pre = dot_nn(rows, w_in[...])
        d_hidden = dot_nn(gexp[...], w_out[...])
        square = pre * pre
        half = 0.5 + 0.5 * jnp.tanh(pre * (COEF + COEF * CUBIC * square))
        hidden = pre * half
        slope = half + hidden * (1.0 - half) * (2.0 * COEF + 6.0 * COEF * CUBIC * square)
        hidden_low = hidden.astype(BF16)
        d_pre = (d_hidden * slope).astype(BF16)
        hid[...] = hidden_low
        dpre[...] = d_pre
        made_sum[...] += dot_nt(hidden_low, w_out[...])
        back_sum[...] += dot_nt(d_pre, w_in[...])

    @pl.when(step == pl.num_programs(0) - 1)
    def _():
        made = made_sum[...]
        made_ref[...] = made.astype(BF16)
        back_ref[:slots, :] = back_sum[...].astype(BF16)
        by_gate = jnp.sum(grads_ref[:slots, :].astype(F32) * made, axis=1, keepdims=True)
        pieces = split_three(jnp.broadcast_to(by_gate, (slots, 128)))
        lane = lax.broadcasted_iota(jnp.int32, (slots, 128), 1)
        stacked = jnp.zeros((slots, 128), F32)
        for index, piece in enumerate(pieces):
            stacked = jnp.where(lane == index, piece.astype(F32), stacked)
        back_ref[slots:, :] = jnp.zeros((TAIL, back_ref.shape[1]), BF16)
        back_ref[slots:, :slots] = stacked.T[:TAIL].astype(BF16)


def expert_chunk(rows, grads, own_in, own_out, other_in, other_out, ahead=()):
    slots, width = rows.shape[0] - TAIL, rows.shape[1]
    half = own_in.shape[1]
    cols = 256
    steps = half // cols
    weights = pl.BlockSpec((width, cols), lambda f: (0, f))
    out = pl.BlockSpec((slots, cols), lambda f: (0, f))
    acts = jax.ShapeDtypeStruct((slots, half), BF16)
    return pl.pallas_call(
        expert_kernel,
        grid=(steps,),
        in_specs=[
            whole((slots + TAIL, width)), whole((slots + TAIL, width)),
            weights, weights, weights, weights,
        ]
        + [ANY] * len(ahead),
        out_specs=[
            out, out, out, out,
            whole((slots + TAIL, width)), whole((slots, width)),
            whole((width, slots)), whole((width, slots)),
        ],
        out_shape=[
            acts, acts, acts, acts,
            jax.ShapeDtypeStruct((slots + TAIL, width), BF16),
            jax.ShapeDtypeStruct((slots, width), BF16),
            jax.ShapeDtypeStruct((width, slots), BF16),
            jax.ShapeDtypeStruct((width, slots), BF16),
        ],
        scratch_shapes=[
            pltpu.VMEM((slots, width), BF16),
            pltpu.VMEM((slots, width), F32),
            pltpu.VMEM((slots, width), F32),
        ],
        compiler_params=pltpu.CompilerParams(vmem_limit_bytes=60 * MIB),
        cost_estimate=LIGHT,
        name="expert_chunk",
    )(rows, grads, own_in, own_out, other_in, other_out, *ahead)


def weight_grad_kernel(count, *refs):
    turned = refs[:count]
    acts = refs[count : 2 * count]
    out_ref = refs[-1]
    total = dot_nn(turned[0][...], acts[0][...])
    for index in range(1, count):
        total = total + dot_nn(turned[index][...], acts[index][...])
    out_ref[...] = total.astype(BF16)


def weight_grad(turned, acts, ahead=()):
    count = len(turned)
    width, slots = turned[0].shape
    half = acts[0].shape[1]
    cols = 512
    return pl.pallas_call(
        functools.partial(weight_grad_kernel, count),
        grid=(half // cols,),
        in_specs=[whole((width, slots))] * count
        + [pl.BlockSpec((slots, cols), lambda f: (0, f))] * count
        + [ANY] * len(ahead),
        out_specs=pl.BlockSpec((width, cols), lambda f: (0, f)),
        out_shape=jax.ShapeDtypeStruct((width, half), BF16),
        compiler_params=pltpu.CompilerParams(vmem_limit_bytes=60 * MIB),
        cost_estimate=LIGHT,
        name="weight_grad",
    )(*turned, *acts, *ahead)


def combine_kernel(count, *refs):
    backs, ends = refs[:count], refs[count : 2 * count]
    (dest_ref, gates_ref, residual_ref, grad_ref, gain_ref, router_ref, w_ref) = refs[
        2 * count : 2 * count + 7
    ]
    (d_residual_ref, branch_ref, mixed_ref, gain_grad, logit_grad, stacked, tails) = refs[-7:]
    slots = backs[0].shape[0]

    @pl.when(pl.program_id(0) == 0)
    def _():
        gain_grad[...] = jnp.zeros_like(gain_grad)
        tails[...] = jnp.zeros_like(tails)
        for index, (back, end) in enumerate(zip(backs, ends)):
            columns = slice(index * slots, (index + 1) * slots)
            stacked[columns, :] = back[...]
            tails[index * TAIL : (index + 1) * TAIL, columns] = end[:, :slots]

    place = lax.broadcasted_iota(jnp.int32, (ROWS, slots), 1)
    lane = lax.broadcasted_iota(jnp.int32, (ROWS, 128), 1)
    hot = jnp.concatenate(
        [
            (place == dest_ref[:, index : index + 1]).astype(F32).astype(BF16)
            for index in range(count)
        ],
        axis=1,
    )
    d_normed = dot_nn(hot, stacked[...])
    picked = dot_nt(hot, tails[...])
    d_gates = jnp.zeros((ROWS, 128), F32)
    for index in range(count):
        part = picked[:, index * TAIL : index * TAIL + 1]
        for extra in (1, 2):
            part = part + picked[:, index * TAIL + extra : index * TAIL + extra + 1]
        d_gates = jnp.where(lane == index, part, d_gates)
    gates = gates_ref[...]
    inner = jnp.sum(gates * d_gates, axis=1, keepdims=True)
    d_logits = gates * (d_gates - inner)
    logit_grad[...] = d_logits
    for index in range(count):
        d_normed = d_normed + d_logits[:, index : index + 1] * router_ref[index : index + 1, :]
    residual = residual_ref[...]
    scale = lax.rsqrt(jnp.mean(residual * residual, axis=1, keepdims=True) + EPS)
    unit = residual * scale
    scaled = gain_ref[...] * d_normed
    pull = jnp.mean(scaled * unit, axis=1, keepdims=True)
    d_residual = grad_ref[...].astype(F32) + scale * (scaled - unit * pull)
    d_residual_ref[...] = d_residual
    branch = d_residual.astype(BF16)
    branch_ref[...] = branch
    mixed_ref[...] = dot_nt(branch, w_ref[...]).astype(BF16)
    gain_grad[...] += jnp.sum(d_normed * unit, axis=0, keepdims=True)


def combine_back(backs, dest_col, gates, residual, grad, gain, router_rows, w_out, ahead=()):
    rows, width = residual.shape
    count = len(backs)
    slots = backs[0].shape[0] - TAIL
    block = lambda n: pl.BlockSpec((ROWS, n), lambda i: (i, 0))
    return pl.pallas_call(
        functools.partial(combine_kernel, count),
        grid=(rows // ROWS,),
        in_specs=[pl.BlockSpec((slots, width), lambda i: (0, 0))] * count
        + [pl.BlockSpec((TAIL, width), lambda i: (slots // TAIL, 0))] * count
        + [
            block(128), block(128), block(width), block(width), whole((1, width)),
            whole(router_rows.shape), whole((width, width)),
        ]
        + [ANY] * len(ahead),
        out_specs=[block(width), block(width), block(width), whole((1, width)), block(128)],
        out_shape=[
            jax.ShapeDtypeStruct((rows, width), F32),
            jax.ShapeDtypeStruct((rows, width), BF16),
            jax.ShapeDtypeStruct((rows, width), BF16),
            jax.ShapeDtypeStruct((1, width), F32),
            jax.ShapeDtypeStruct((rows, 128), F32),
        ],
        scratch_shapes=[
            pltpu.VMEM((count * slots, width), BF16),
            pltpu.VMEM((count * TAIL, count * slots), BF16),
        ],
        compiler_params=pltpu.CompilerParams(vmem_limit_bytes=48 * MIB),
        cost_estimate=LIGHT,
        name="combine_back",
    )(*backs, *backs, dest_col, gates, residual, grad, gain, router_rows, w_out, *ahead)


def output_kernel(count, *refs):
    mades = refs[:count]
    dest_ref, gates_ref, residual_ref = refs[count : count + 3]
    out_ref = refs[-1]
    slots = mades[0].shape[0]
    place = lax.broadcasted_iota(jnp.int32, (ROWS, slots), 1)
    total = residual_ref[...]
    for index, made in enumerate(mades):
        hot = (place == dest_ref[:, index : index + 1]).astype(F32).astype(BF16)
        total = total + gates_ref[:, index : index + 1] * dot_nn(hot, made[...])
    out_ref[...] = total.astype(BF16)


def combine_output(mades, dest_col, gates, residual, ahead=()):
    rows, width = residual.shape
    count = len(mades)
    slots = mades[0].shape[0]
    block = lambda n: pl.BlockSpec((ROWS, n), lambda i: (i, 0))
    return pl.pallas_call(
        functools.partial(output_kernel, count),
        grid=(rows // ROWS,),
        in_specs=[pl.BlockSpec((slots, width), lambda i: (0, 0))] * count
        + [block(128), block(128), block(width)]
        + [ANY] * len(ahead),
        out_specs=block(width),
        out_shape=jax.ShapeDtypeStruct((rows, width), BF16),
        compiler_params=pltpu.CompilerParams(vmem_limit_bytes=40 * MIB),
        cost_estimate=LIGHT,
        name="combine_output",
    )(*mades, dest_col, gates, residual, *ahead)


def final_kernel(dqkv_ref, w_ref, tokens_ref, gain_ref, d_residual_ref, *rest):
    out_ref = rest[-1]
    width = tokens_ref.shape[1]
    d_normed = (
        dot_nt(dqkv_ref[0], w_ref[:, :width])
        + dot_nt(dqkv_ref[1], w_ref[:, width : 2 * width])
        + dot_nt(dqkv_ref[2], w_ref[:, 2 * width : 3 * width])
    )
    tokens = tokens_ref[...].astype(F32)
    scale = lax.rsqrt(jnp.mean(tokens * tokens, axis=1, keepdims=True) + EPS)
    unit = tokens * scale
    scaled = gain_ref[...] * d_normed
    pull = jnp.mean(scaled * unit, axis=1, keepdims=True)
    out_ref[...] = d_residual_ref[...] + scale * (scaled - unit * pull)


def final_tokens(d_qkv, w_all, tokens, gain, d_residual, ahead=()):
    rows, width = tokens.shape
    block = lambda n: pl.BlockSpec((ROWS, n), lambda i: (i, 0))
    return pl.pallas_call(
        final_kernel,
        grid=(rows // ROWS,),
        in_specs=[
            pl.BlockSpec((3, ROWS, width), lambda i: (0, i, 0)), whole((width, 3 * width)),
            block(width), whole((1, width)), block(width),
        ]
        + [ANY] * len(ahead),
        out_specs=block(width),
        out_shape=jax.ShapeDtypeStruct((rows, width), F32),
        compiler_params=pltpu.CompilerParams(vmem_limit_bytes=40 * MIB),
        cost_estimate=LIGHT,
        name="final_tokens",
    )(d_qkv, w_all, tokens, gain, d_residual, *ahead)


def qkv_grad_kernel(parts, turned_ref, grad_ref, mixed_ref, branch_ref, extra_ref, *rest):
    step = pl.program_id(0)
    keep_ref, send_ref = rest[-2:]
    half = keep_ref.shape[0]

    def store(made):
        keep_ref[...] = made[:half]
        send_ref[...] = made[half:]

    @pl.when(step < 3 * parts)
    def _():
        store(dot_nn(turned_ref[...], grad_ref[0]).astype(BF16))

    @pl.when((step >= 3 * parts) & (step < 4 * parts))
    def _():
        store(dot_nn(mixed_ref[...], branch_ref[...]).astype(BF16))

    @pl.when(step == 4 * parts)
    def _():
        store(extra_ref[...])


def qkv_grad(turned, d_qkv, mixed_turned, branch, extra, ahead=()):
    width, rows = turned.shape
    parts = width // BLK

    def place(j):
        j = jnp.minimum(j, 3 * parts - 1)
        return (j // parts, 0, j % parts)

    def place_branch(j):
        return (0, jnp.clip(j - 3 * parts, 0, parts - 1))

    return pl.pallas_call(
        functools.partial(qkv_grad_kernel, parts),
        grid=(4 * parts + 1,),
        in_specs=[
            whole((width, rows)), pl.BlockSpec((1, rows, BLK), place),
            whole((width, rows)), pl.BlockSpec((rows, BLK), place_branch), whole((width, BLK)),
        ]
        + [ANY] * len(ahead),
        out_specs=[pl.BlockSpec((width // 2, BLK), lambda j: (0, j))] * 2,
        out_shape=[jax.ShapeDtypeStruct((width // 2, 4 * width + BLK), BF16)] * 2,
        compiler_params=pltpu.CompilerParams(vmem_limit_bytes=40 * MIB),
        cost_estimate=LIGHT,
        name="qkv_grad",
    )(turned, d_qkv, mixed_turned, branch, extra, *ahead)


def pairs_of(size, offset):
    return [(i, i ^ offset) for i in range(size)]


def gather_rows(block, ahead):
    dp_size, fsdp_size = lax.axis_size("dp"), lax.axis_size("fsdp")
    line = [block]
    for m in range(1, dp_size):
        line.append(lax.ppermute(block, "dp", pairs_of(dp_size, m)))
    line = jnp.concatenate(line, axis=0)
    plane = [line]
    for m in range(1, fsdp_size // 2):
        plane.append(lax.ppermute(line, "fsdp", pairs_of(fsdp_size, 2 * m)))
    (plane,) = held([jnp.concatenate(plane, axis=0)], ahead)
    other = lax.ppermute(plane, "fsdp", pairs_of(fsdp_size, 1))
    return plane, jnp.concatenate([plane, other], axis=0)


def scatter_pair(keep, send):
    fsdp_size = lax.axis_size("fsdp")
    got = lax.ppermute(send, "fsdp", pairs_of(fsdp_size, 1))
    return (keep.astype(F32) + got.astype(F32)).astype(BF16)


def scatter_plane(plane):
    fsdp_size = lax.axis_size("fsdp")
    rows = 2 * plane.shape[0] // fsdp_size
    line = plane[:rows].astype(F32)
    for m in range(1, fsdp_size // 2):
        got = lax.ppermute(plane[m * rows : (m + 1) * rows], "fsdp", pairs_of(fsdp_size, 2 * m))
        line = line + got.astype(F32)
    return line.astype(BF16)


def scatter_line(line):
    dp_size = lax.axis_size("dp")
    rows = line.shape[0] // dp_size
    total = line[:rows].astype(F32)
    for m in range(1, dp_size):
        got = lax.ppermute(line[m * rows : (m + 1) * rows], "dp", pairs_of(dp_size, m))
        total = total + got.astype(F32)
    return total


def position_matrix(width):
    dp_size, fsdp_size = lax.axis_size("dp"), lax.axis_size("fsdp")
    layer, place = lax.axis_index("dp"), lax.axis_index("fsdp")
    chips = fsdp_size // 2
    rows = width // (dp_size * fsdp_size)
    position = jnp.arange(width, dtype=jnp.int32)
    row = position % rows
    layer_of = (position // rows) % dp_size ^ layer
    chip_of = (position // (rows * dp_size)) % chips ^ (place // 2)
    core_of = position // (rows * dp_size * chips) ^ (place % 2)
    source = ((layer_of * chips + chip_of) * 2 + core_of) * rows + row
    return (position[:, None] == source[None, :]).astype(BF16)


def local(
    tokens_in, w_qkv, w_attn_out, gain_attn, gain_ffn, rel_bias, router, w_in, w_out,
    segment_ids, expert_ids, d_out,
):
    tok_rows, width = tokens_in.shape
    top_count = expert_ids.shape[1]
    fsdp_size = lax.axis_size("fsdp")
    experts = fsdp_size // 2
    slots = min(tok_rows, tok_rows * top_count * 5 // (4 * experts))
    me = lax.axis_index("fsdp") // 2

    own_in = lax.all_gather(w_in, "dp", axis=0, tiled=True)
    own_out = lax.all_gather(w_out, "dp", axis=0, tiled=True)
    small = jnp.concatenate(
        [router, gain_attn[:, None], gain_ffn[:, None], rel_bias[:, None]], axis=1
    )
    small = jnp.pad(small, ((0, 0), (0, 128 - small.shape[1])))
    relative = expert_ids ^ me
    hot = jnp.sum(
        (relative[:, :, None] == jnp.arange(experts, dtype=jnp.int32)).astype(jnp.int32), axis=1
    )
    rank = jnp.cumsum(hot, axis=0) - hot
    dest = jnp.where(hot > 0, rank, -1)
    dest_col = jnp.pad(dest, ((0, 0), (0, 128 - experts)), constant_values=-1)
    dest_row = dest.T.reshape(experts, 1, tok_rows)

    def exchange(pieces):
        return [pieces[0]] + [
            lax.ppermute(pieces[m], "fsdp", pairs_of(fsdp_size, 2 * m)) for m in range(1, experts)
        ]

    sent_grads = dispatch(dest_row, d_out, jnp.zeros((experts, 1, tok_rows), F32), slots)
    move = position_matrix(width)
    moved_tokens = jnp.dot(tokens_in, move, preferred_element_type=F32)
    plane, full = gather_rows(
        jnp.concatenate([w_qkv, w_attn_out, small], axis=1), tuple(sent_grads[1:2])
    )
    grads_in = exchange([sent_grads[0]] + list(held(sent_grads[1:], (plane,))))

    moved_gain = full[:, 4 * width + experts].astype(F32).reshape(1, width)
    columns = jnp.dot(move, full[:, 4 * width :], preferred_element_type=F32).astype(BF16)
    back_qkv = jnp.dot(move, full[:, : 3 * width], preferred_element_type=F32).astype(BF16)
    back_attn = jnp.dot(
        move, full[:, 3 * width : 4 * width], preferred_element_type=F32
    ).astype(BF16)
    by_row = columns.T
    gain_a = by_row[experts : experts + 1].astype(F32)
    gain_f = by_row[experts + 1 : experts + 2].astype(F32)
    table = by_row[experts + 2].reshape(HEADS, BUCKETS)
    bucket_hot = (
        buckets_of(jnp.arange(BLK, dtype=jnp.int32))[:, None]
        == jnp.arange(BUCKETS, dtype=jnp.int32)[None, :]
    )
    near = jnp.dot(table, bucket_hot.T.astype(BF16), preferred_element_type=F32)
    near = near.reshape(HEADS // 2, 2, BLK)
    far = table[:, BUCKETS - 1].astype(F32)
    place = jnp.arange(128, dtype=jnp.int32)
    swap = ((place[:, None] ^ me) == place[None, :]) & (place[:, None] < experts)
    router_cols = jnp.dot(columns, swap.astype(BF16), preferred_element_type=F32).astype(BF16)
    router_rows = router_cols.T[: max(8, experts)].astype(F32)

    tokens = tokens_in.astype(F32)
    scale = lax.rsqrt(jnp.mean(tokens * tokens, axis=1, keepdims=True) + EPS)
    normed_attn = (moved_tokens * scale * moved_gain).astype(BF16)
    qkv_rows = jnp.dot(normed_attn, full[:, : 3 * width], preferred_element_type=F32).astype(BF16)
    segments = segment_ids.reshape(tok_rows)
    mixed, lse = attention_forward(
        qkv_rows, segments, near, far, HEADS, tuple(grads_in[1:3])
    )
    residual, normed_ffn, gates, moved_mixed = post_attention(
        mixed, full, tokens_in, gain_f, router_cols, dest_col, move
    )
    gate_row = gates[:, :experts].T.reshape(experts, 1, tok_rows)
    sent_rows = dispatch(dest_row, normed_ffn, gate_row, slots)
    rows_in = exchange(sent_rows)
    (own_in,) = held([own_in], (mixed,))
    (own_out,) = held([own_out], (sent_rows[0],))
    other_in = lax.ppermute(own_in, "fsdp", pairs_of(fsdp_size, 1))
    other_out = lax.ppermute(own_out, "fsdp", pairs_of(fsdp_size, 1))

    chunks, backs = [], []
    for m in range(experts):
        ahead = tuple(backs[1 : m - 1]) + ((chunks[-1][4],) if chunks else ())
        chunks.append(
            expert_chunk(rows_in[m], grads_in[m], own_in, own_out, other_in, other_out, ahead)
        )
        back = chunks[-1][4]
        backs.append(
            lax.ppermute(back, "fsdp", pairs_of(fsdp_size, 2 * m)) if m > 0 else back
        )
    hid_own, hid_other, dpre_own, dpre_other, _, made, rows_turned, gexp_turned = zip(*chunks)
    mades = exchange(made)

    def pair_sum(own, other):
        got = lax.ppermute(other, "fsdp", pairs_of(fsdp_size, 1))
        return (own.astype(F32) + got.astype(F32)).astype(BF16)

    def owners(pair):
        return lax.psum_scatter(pair, "dp", scatter_dimension=0, tiled=True).astype(F32)

    grad_in_own = weight_grad(rows_turned, dpre_own, tuple(backs[-2:-1]))
    grad_out_own = weight_grad(gexp_turned, hid_own, (grad_in_own,))
    grad_in_other = weight_grad(rows_turned, dpre_other, (grad_out_own,) + tuple(backs[-1:]))
    grad_out_other = weight_grad(gexp_turned, hid_other, (grad_in_other,))
    pair_in = pair_sum(grad_in_own, grad_in_other)
    pair_out = pair_sum(grad_out_own, grad_out_other)
    d_w_in, d_w_out = owners(pair_in), owners(pair_out)

    d_residual, d_branch, d_mixed, d_gain_f, d_logits = combine_back(
        backs, dest_col, gates, residual, d_out, gain_f, router_rows, back_attn, (grad_out_other, pair_in)
    )
    d_qkv, near_grad, far_grad = attention_backward(
        qkv_rows, d_mixed, mixed, lse, segments, near, far, HEADS, (pair_out,)
    )
    d_router = jnp.dot(normed_ffn.T, d_logits.astype(BF16), preferred_element_type=F32)
    d_router = jnp.dot(d_router, swap.T.astype(F32), precision=lax.Precision.HIGHEST)
    d_table = jnp.dot(
        near_grad.reshape(HEADS, BLK), bucket_hot.astype(F32), precision=lax.Precision.HIGHEST
    )
    last = jnp.arange(BUCKETS, dtype=jnp.int32)[None, :] == BUCKETS - 1
    d_table = d_table + jnp.where(last, far_grad[:, :, :1].reshape(HEADS, 1), 0.0)
    late_cols = jnp.where(place[None, :] == experts, d_gain_f.reshape(width, 1), d_router)
    late_cols = jnp.where(place[None, :] == experts + 1, d_table.reshape(width, 1), late_cols)
    late_cols = jnp.dot(move.T, late_cols.astype(BF16), preferred_element_type=F32)
    late_cols = jnp.pad(late_cols.astype(BF16), ((0, 0), (0, BLK - 128)))
    keep, send = qkv_grad(
        normed_attn.T, d_qkv, moved_mixed.T, d_branch, late_cols, (d_w_in,) + tuple(mades[1:])
    )
    late = scatter_line(scatter_plane(scatter_pair(keep, send)))
    block_out = combine_output(mades, dest_col, gates, residual, (keep,))
    d_tokens = final_tokens(d_qkv, back_qkv, tokens_in, gain_a, d_residual, (d_w_out,))
    own_qkv = late[:, : 3 * width]
    own_gain_a = jnp.sum(own_qkv * w_qkv.astype(F32), axis=1) / gain_attn.astype(F32)
    return (
        block_out,
        d_tokens,
        own_qkv,
        late[:, 3 * width : 4 * width],
        own_gain_a,
        late[:, 4 * width + experts],
        late[:, 4 * width + experts + 1],
        late[:, 4 * width : 4 * width + experts],
        d_w_in,
        d_w_out,
    )


def solution(mesh):
    both = P(("dp", "fsdp"), None)
    line = P(("dp", "fsdp"))
    tiles = P("dp", "fsdp")
    return jax.shard_map(
        local,
        mesh=mesh,
        in_specs=(both, both, both, line, line, line, both, tiles, tiles, both, both, both),
        out_specs=(both, both, both, both, line, line, line, both, tiles, tiles),
        check_vma=False,
    )
```

```python
import functools
import math

import jax
import jax.numpy as jnp
from jax import lax
from jax.experimental import pallas as pl
from jax.experimental.pallas import tpu as pltpu
from jax.sharding import PartitionSpec as P

NEG = -1e30
BLK = 256
SPAN = 2
F32 = jnp.float32
BF16 = jnp.bfloat16
LIGHT = pl.CostEstimate(flops=1000, bytes_accessed=1000, transcendentals=0)


def dot_nt(a, b):
    return lax.dot_general(a, b, (((1,), (1,)), ((), ())), preferred_element_type=F32)


def dot_nn(a, b):
    return lax.dot_general(a, b, (((1,), (0,)), ((), ())), preferred_element_type=F32)


def fill_masks(mask, seg_row, seg_col, blocks):
    key_place = lax.broadcasted_iota(jnp.int32, (BLK, BLK), 0)
    row_place = lax.broadcasted_iota(jnp.int32, (BLK, BLK), 1)
    for kb in range(blocks):
        keys = seg_col[kb * BLK : (kb + 1) * BLK, :]
        for step in range(min(SPAN + 1, blocks - kb)):
            rows = seg_row[:, (kb + step) * BLK : (kb + step + 1) * BLK]
            seen = keys == rows
            if step == 0:
                seen = seen & (row_place >= key_place)
            mask[kb, step] = jnp.where(seen, 0.0, NEG)


def bias_tiles(near_row, far_value):
    key_place = lax.broadcasted_iota(jnp.int32, (BLK, BLK), 0)
    row_place = lax.broadcasted_iota(jnp.int32, (BLK, BLK), 1)
    rolled = pltpu.roll(
        jnp.broadcast_to(near_row, (BLK, BLK)), 0, 1, stride=1, stride_axis=0
    )
    return rolled, jnp.where(row_place < key_place, rolled, far_value)


def head_lanes(values, half):
    lane = lax.broadcasted_iota(jnp.int32, values.shape, 1)
    keep = (lane >= 64) if half else (lane < 64)
    return jnp.where(keep, values, jnp.zeros_like(values))


def attn_fwd_kernel(
    far_ref, q_ref, k_ref, v_ref, near_ref, seg_row, seg_col, *rest
):
    o_ref, lse_ref, mask, turned = rest[-4:]
    pair = pl.program_id(0)
    length = q_ref.shape[0]
    blocks = length // BLK

    @pl.when(pair == 0)
    def _():
        fill_masks(mask, seg_row, seg_col, blocks)

    v_turned = v_ref[...].T
    ones = jnp.ones((16, length), BF16)
    for half in range(2):
        far_value = far_ref[pair * 2 + half]
        diag, below = bias_tiles(near_ref[0, half : half + 1, :], far_value)
        keys = head_lanes(k_ref[...], half)
        values = jnp.concatenate([v_turned[64 * half : 64 * half + 64], ones], axis=0)
        for a in range(blocks):
            first = max(0, a - SPAN)
            q_rows = q_ref[a * BLK : (a + 1) * BLK, :] * jnp.asarray(0.125, BF16)
            parts = []
            for kb in range(first, a + 1):
                part = dot_nt(keys[kb * BLK : (kb + 1) * BLK], q_rows)
                bias = (diag, below, far_value)[a - kb]
                parts.append(part + bias + mask[kb, a - kb])
            peak = functools.reduce(
                jnp.maximum, [jnp.max(part, axis=0, keepdims=True) for part in parts]
            )
            weights = jnp.concatenate(
                [jnp.exp(part - peak).astype(BF16) for part in parts], axis=0
            )
            made = dot_nn(values[:, first * BLK : (a + 1) * BLK], weights)
            total = made[64:65]
            turned[64 * half : 64 * half + 64, a * BLK : (a + 1) * BLK] = made[:64] / total
            lse_ref[0, half : half + 1, a * BLK : (a + 1) * BLK] = peak + jnp.log(total)
    o_ref[...] = turned[...].T.astype(BF16)


def attn_bwd_kernel(
    far_ref, q_ref, k_ref, v_ref, g_ref, o_ref, lse_ref, near_ref, seg_row, seg_col, *rest
):
    d_ref, near_grad, far_grad, mask, turned = rest[-5:]
    pair = pl.program_id(0)
    length = q_ref.shape[0]
    blocks = length // BLK

    @pl.when(pair == 0)
    def _():
        fill_masks(mask, seg_row, seg_col, blocks)

    scaled = q_ref[...] * jnp.asarray(0.125, BF16)
    k_turned = k_ref[...].T
    ones = jnp.ones((16, length), BF16)
    inner = (g_ref[...].astype(F32) * o_ref[...].astype(F32)).T
    key_place = lax.broadcasted_iota(jnp.int32, (BLK, BLK), 0)
    row_place = lax.broadcasted_iota(jnp.int32, (BLK, BLK), 1)
    key_grads = [None] * blocks
    value_grads = [None] * blocks
    for half in range(2):
        far_value = far_ref[pair * 2 + half]
        diag, below = bias_tiles(near_ref[0, half : half + 1, :], far_value)
        keys = head_lanes(k_ref[...], half)
        values = head_lanes(v_ref[...], half)
        q_own = head_lanes(scaled, half)
        g_own = head_lanes(g_ref[...], half)
        keys_turned = jnp.concatenate([k_turned[64 * half : 64 * half + 64], ones], axis=0)
        delta = jnp.sum(inner[64 * half : 64 * half + 64], axis=0, keepdims=True)
        lse = lse_ref[0, half : half + 1, :]
        diag_grad = jnp.zeros((BLK, BLK), F32)
        below_grad = jnp.zeros((BLK, BLK), F32)
        turned[...] = jnp.zeros_like(turned)
        for kb in range(blocks):
            last = min(kb + SPAN + 1, blocks)
            k_rows = keys[kb * BLK : (kb + 1) * BLK]
            v_rows = values[kb * BLK : (kb + 1) * BLK]
            probs, grads = [], []
            for a in range(kb, last):
                rows = slice(a * BLK, (a + 1) * BLK)
                score = dot_nt(k_rows, scaled[rows])
                d_prob = dot_nt(v_rows, g_ref[rows, :])
                bias = (diag, below, far_value)[a - kb]
                prob = jnp.exp(score + bias + mask[kb, a - kb] - lse[:, rows])
                d_score = prob * (d_prob - delta[:, rows])
                if a == kb:
                    diag_grad = diag_grad + d_score
                elif a == kb + 1:
                    below_grad = below_grad + d_score
                probs.append(prob.astype(BF16))
                grads.append(d_score.astype(BF16))
            wide = slice(kb * BLK, last * BLK)
            prob_wide = jnp.concatenate(probs, axis=1)
            grad_wide = jnp.concatenate(grads, axis=1)
            value_grad = dot_nn(prob_wide, g_own[wide])
            key_grad = dot_nn(grad_wide, q_own[wide])
            turned[:, wide] += dot_nn(keys_turned[:, kb * BLK : (kb + 1) * BLK], grad_wide)
            if half == 0:
                value_grads[kb], key_grads[kb] = value_grad, key_grad
            else:
                rows = slice(kb * BLK, (kb + 1) * BLK)
                d_ref[2, rows, :] = (value_grads[kb] + value_grad).astype(BF16)
                d_ref[1, rows, :] = (key_grads[kb] + key_grad).astype(BF16)
        part = (turned[:64] * 0.125).T
        if half == 0:
            first_part = part
        else:
            d_ref[0] = jnp.concatenate([first_part, part], axis=1).astype(BF16)
        by_offset = diag_grad + jnp.where(row_place < key_place, below_grad, 0.0)
        for bit in range(8):
            by_offset = jnp.where(
                ((key_place >> bit) & 1) == 1,
                pltpu.roll(by_offset, BLK - (1 << bit), 1),
                by_offset,
            )
        near = jnp.sum(by_offset, axis=0, keepdims=True)
        near_grad[0, half : half + 1, :] = near
        everything = jnp.sum(turned[64:65, :], axis=1, keepdims=True)
        rest = everything - jnp.sum(near, axis=1, keepdims=True)
        far_grad[0, half : half + 1, :] = jnp.broadcast_to(rest, (1, 128))


def attention_specs(length, pairs):
    def column(offset):
        return pl.BlockSpec((length, 128), lambda p, far: (0, p + offset))

    return column


def attention_forward(qkv_rows, segments, near, far, heads, ahead=()):
    length = qkv_rows.shape[0]
    pairs = heads // 2
    width = heads * 64
    column = attention_specs(length, pairs)
    blocks = length // BLK
    return pl.pallas_call(
        attn_fwd_kernel,
        grid_spec=pltpu.PrefetchScalarGridSpec(
            num_scalar_prefetch=1,
            grid=(pairs,),
            in_specs=[
                column(0),
                column(pairs),
                column(2 * pairs),
                pl.BlockSpec((1, 2, BLK), lambda p, far: (p, 0, 0)),
                pl.BlockSpec((1, length), lambda p, far: (0, 0)),
                pl.BlockSpec((length, 1), lambda p, far: (0, 0)),
            ]
            + [pl.BlockSpec(memory_space=pl.ANY)] * len(ahead),
            out_specs=[
                column(0),
                pl.BlockSpec((1, 2, length), lambda p, far: (p, 0, 0)),
            ],
            scratch_shapes=[
                pltpu.VMEM((blocks, SPAN + 1, BLK, BLK), F32),
                pltpu.VMEM((128, length), F32),
            ],
        ),
        out_shape=[
            jax.ShapeDtypeStruct((length, width), BF16),
            jax.ShapeDtypeStruct((pairs, 2, length), F32),
        ],
        compiler_params=pltpu.CompilerParams(vmem_limit_bytes=60 * 1024 * 1024),
        cost_estimate=LIGHT,
        name="attention_forward",
    )(far, qkv_rows, qkv_rows, qkv_rows, near, segments.reshape(1, length), segments.reshape(length, 1), *ahead)


def attention_backward(qkv_rows, d_mixed, mixed, lse, segments, near, far, heads, ahead=()):
    length = qkv_rows.shape[0]
    pairs = heads // 2
    width = heads * 64
    column = attention_specs(length, pairs)
    blocks = length // BLK
    small = lambda n: pl.BlockSpec((1, 2, n), lambda p, far: (p, 0, 0))
    return pl.pallas_call(
        attn_bwd_kernel,
        grid_spec=pltpu.PrefetchScalarGridSpec(
            num_scalar_prefetch=1,
            grid=(pairs,),
            in_specs=[
                column(0),
                column(pairs),
                column(2 * pairs),
                column(0),
                column(0),
                small(length),
                small(BLK),
                pl.BlockSpec((1, length), lambda p, far: (0, 0)),
                pl.BlockSpec((length, 1), lambda p, far: (0, 0)),
            ]
            + [pl.BlockSpec(memory_space=pl.ANY)] * len(ahead),
            out_specs=[
                pl.BlockSpec((3, length, 128), lambda p, far: (0, 0, p)),
                small(BLK),
                small(128),
            ],
            scratch_shapes=[
                pltpu.VMEM((blocks, SPAN + 1, BLK, BLK), F32),
                pltpu.VMEM((80, length), F32),
            ],
        ),
        out_shape=[
            jax.ShapeDtypeStruct((3, length, width), BF16),
            jax.ShapeDtypeStruct((pairs, 2, BLK), F32),
            jax.ShapeDtypeStruct((pairs, 2, 128), F32),
        ],
        compiler_params=pltpu.CompilerParams(vmem_limit_bytes=60 * 1024 * 1024),
        cost_estimate=LIGHT,
        name="attention_backward",
    )(
        far, qkv_rows, qkv_rows, qkv_rows, d_mixed, mixed, lse, near,
        segments.reshape(1, length), segments.reshape(length, 1), *ahead,
    )


HEADS = 12
BUCKETS = 64
MAX_DIST = 128
EPS = 1e-06
ROWS = 256
TAIL = 16
COEF = math.sqrt(2.0 / math.pi)
CUBIC = 0.044715
MIB = 1024 * 1024


def bucket_bounds(bucket_count, max_distance):
    halfway = bucket_count // 2
    bounds = []
    for bucket in range(bucket_count):
        if bucket < halfway:
            bounds.append(bucket)
        else:
            bounds.append(
                int(math.ceil(halfway * (max_distance / halfway) ** ((bucket - halfway) / halfway)))
            )
    return bounds


def buckets_of(distance):
    limits = jnp.array(bucket_bounds(BUCKETS, MAX_DIST), dtype=jnp.int32)
    reached = (distance[:, None] >= limits[None, :]).astype(jnp.int32)
    return jnp.sum(reached, axis=1) - 1


def whole(shape):
    return pl.BlockSpec(shape, lambda *_: (0,) * len(shape))


def split_three(values):
    high = values.astype(BF16)
    rest = values - high.astype(F32)
    middle = rest.astype(BF16)
    low = (rest - middle.astype(F32)).astype(BF16)
    return high, middle, low


ANY = pl.BlockSpec(memory_space=pl.ANY)


def dispatch_kernel(experts, dest_ref, values_ref, gate_ref, *rest):
    out_refs = rest[-experts:]
    slots = out_refs[0].shape[0] - TAIL
    tokens = values_ref.shape[0]
    own = pl.ds(pl.program_id(0), 1)
    place = lax.broadcasted_iota(jnp.int32, (slots, tokens), 0)
    hot = (place == dest_ref[own, :]).astype(F32).astype(BF16)
    rows = dot_nn(hot, values_ref[...]).astype(BF16)
    pieces = split_three(jnp.broadcast_to(gate_ref[own, :], (TAIL, tokens)))
    line = lax.broadcasted_iota(jnp.int32, (TAIL, tokens), 0)
    stacked = jnp.zeros((TAIL, tokens), F32)
    for index, piece in enumerate(pieces):
        stacked = jnp.where(line == index, piece.astype(F32), stacked)
    tail = dot_nt(stacked.astype(BF16), hot).astype(BF16)
    for index, out_ref in enumerate(out_refs):

        @pl.when(pl.program_id(0) == index)
        def _():
            out_ref[:slots, :] = rows
            out_ref[slots:, :] = jnp.zeros((TAIL, out_ref.shape[1]), BF16)
            out_ref[slots:, :slots] = tail


def dispatch(experts, dest_row, values, gate_row, slots, ahead=()):
    tokens, width = values.shape
    return pl.pallas_call(
        functools.partial(dispatch_kernel, experts),
        grid=(experts,),
        in_specs=[
            whole(dest_row.shape), whole((tokens, width)), whole(gate_row.shape),
        ]
        + [ANY] * len(ahead),
        out_specs=[whole((slots + TAIL, width))] * experts,
        out_shape=[jax.ShapeDtypeStruct((slots + TAIL, width), BF16)] * experts,
        compiler_params=pltpu.CompilerParams(vmem_limit_bytes=60 * MIB),
        cost_estimate=LIGHT,
        name="dispatch_rows",
    )(dest_row, values, gate_row, *ahead)


def nothing_kernel(*refs):
    pass


def held(values, ahead):
    count = len(values)
    return pl.pallas_call(
        nothing_kernel,
        in_specs=[ANY] * (count + len(ahead)),
        out_specs=[ANY] * count,
        out_shape=[jax.ShapeDtypeStruct(value.shape, value.dtype) for value in values],
        input_output_aliases={index: index for index in range(count)},
        cost_estimate=LIGHT,
        name="held",
    )(*values, *ahead)


def as_columns(ref):
    rows = ref[...].astype(F32)
    filler = jnp.full((128 - rows.shape[0], rows.shape[1]), -1.0, F32)
    return jnp.concatenate([rows, filler], axis=0).T.astype(jnp.int32)


def post_kernel(
    mixed_ref, w_ref, w_rest, tokens_ref, gain_ref, router_ref, dest_ref, move_ref, *rest
):
    residual_ref, normed_ref, gates_ref, turned_ref, moved_ref = rest[-5:]
    half = w_ref.shape[0]
    moved = dot_nn(mixed_ref[...], move_ref[...]).astype(BF16)
    moved_ref[...] = moved
    residual = dot_nn(moved[:, :half], w_ref[...]) + dot_nn(moved[:, half:], w_rest[...])
    residual = tokens_ref[...].astype(F32) + residual
    residual_ref[...] = residual
    scale = lax.rsqrt(jnp.mean(residual * residual, axis=1, keepdims=True) + EPS)
    normed = (residual * scale * gain_ref[...]).astype(BF16)
    normed_ref[...] = normed
    logits = dot_nn(normed, router_ref[...])
    chosen = as_columns(dest_ref) >= 0
    logits = jnp.where(chosen, logits, NEG)
    peak = jnp.max(logits, axis=1, keepdims=True)
    weights = jnp.where(chosen, jnp.exp(logits - peak), 0.0)
    gates = weights / jnp.sum(weights, axis=1, keepdims=True)
    gates_ref[...] = gates
    turned_ref[...] = gates.T[: turned_ref.shape[0]]


def post_attention(mixed, w_top, w_rest, tokens, gain, router, dest_row, move, ahead=()):
    rows, width = tokens.shape
    lines = dest_row.shape[0]
    block = lambda n: pl.BlockSpec((ROWS, n), lambda i: (i, 0))
    return pl.pallas_call(
        post_kernel,
        grid=(rows // ROWS,),
        in_specs=[
            block(width), pl.BlockSpec((width // 2, width), lambda i: (0, 3)),
            pl.BlockSpec((width // 2, width), lambda i: (0, 3)), block(width),
            whole((1, width)), whole((width, 128)),
            pl.BlockSpec((lines, ROWS), lambda i: (0, i)), whole((width, width)),
        ]
        + [ANY] * len(ahead),
        out_specs=[
            block(width), block(width), block(128),
            pl.BlockSpec((lines, ROWS), lambda i: (0, i)), block(width),
        ],
        out_shape=[
            jax.ShapeDtypeStruct((rows, width), F32),
            jax.ShapeDtypeStruct((rows, width), BF16),
            jax.ShapeDtypeStruct((rows, 128), F32),
            jax.ShapeDtypeStruct((lines, rows), F32),
            jax.ShapeDtypeStruct((rows, width), BF16),
        ],
        compiler_params=pltpu.CompilerParams(vmem_limit_bytes=60 * MIB),
        cost_estimate=LIGHT,
        name="post_attention",
    )(mixed, w_top, w_rest, tokens, gain, router, dest_row, move, *ahead)


def expert_kernel(
    rows_ref, grads_ref, in_own, out_own, in_other, out_other, *rest
):
    hid_own, hid_other, dpre_own, dpre_other, back_ref, made_ref = rest[-11:-5]
    rows_turned, gexp_turned, gexp, made_sum, back_sum = rest[-5:]
    step = pl.program_id(0)
    slots = gexp.shape[0]

    @pl.when(step == 0)
    def _():
        turned = rows_ref[slots:, :slots].astype(F32).T
        gate = jnp.sum(turned, axis=1, keepdims=True)
        gexp[...] = (grads_ref[:slots, :].astype(F32) * gate).astype(BF16)
        gexp_turned[...] = gexp[...].T
        rows_turned[...] = rows_ref[:slots, :].T
        made_sum[...] = jnp.zeros_like(made_sum)
        back_sum[...] = jnp.zeros_like(back_sum)

    rows = rows_ref[:slots, :]
    hiddens, d_pres = [], []
    for w_in, w_out, hid, dpre in (
        (in_own, out_own, hid_own, dpre_own),
        (in_other, out_other, hid_other, dpre_other),
    ):
        pre = dot_nn(rows, w_in[...])
        d_hidden = dot_nn(gexp[...], w_out[...])
        square = pre * pre
        half = 0.5 + 0.5 * jnp.tanh(pre * (COEF + COEF * CUBIC * square))
        hidden = pre * half
        slope = half + hidden * (1.0 - half) * (2.0 * COEF + 6.0 * COEF * CUBIC * square)
        hidden_low = hidden.astype(BF16)
        d_pre = (d_hidden * slope).astype(BF16)
        hid[...] = hidden_low
        dpre[...] = d_pre
        hiddens.append(hidden_low)
        d_pres.append(d_pre)
    both_out = jnp.concatenate([out_own[...], out_other[...]], axis=1)
    both_in = jnp.concatenate([in_own[...], in_other[...]], axis=1)
    made_sum[...] += dot_nt(jnp.concatenate(hiddens, axis=1), both_out)
    back_sum[...] += dot_nt(jnp.concatenate(d_pres, axis=1), both_in)

    @pl.when(step == pl.num_programs(0) - 1)
    def _():
        made = made_sum[...]
        made_ref[...] = made.astype(BF16)
        back_ref[:slots, :] = back_sum[...].astype(BF16)
        by_gate = jnp.sum(grads_ref[:slots, :].astype(F32) * made, axis=1, keepdims=True)
        pieces = split_three(jnp.broadcast_to(by_gate, (slots, 128)))
        lane = lax.broadcasted_iota(jnp.int32, (slots, 128), 1)
        stacked = jnp.zeros((slots, 128), F32)
        for index, piece in enumerate(pieces):
            stacked = jnp.where(lane == index, piece.astype(F32), stacked)
        back_ref[slots:, :] = jnp.zeros((TAIL, back_ref.shape[1]), BF16)
        back_ref[slots:, :slots] = stacked.T[:TAIL].astype(BF16)


def expert_chunk(rows, grads, own_in, own_out, other_in, other_out, ahead=()):
    slots, width = rows.shape[0] - TAIL, rows.shape[1]
    half = own_in.shape[1]
    cols = 256
    steps = half // cols
    weights = pl.BlockSpec((width, cols), lambda f: (0, f))
    out = pl.BlockSpec((slots, cols), lambda f: (0, f))
    acts = jax.ShapeDtypeStruct((slots, half), BF16)
    return pl.pallas_call(
        expert_kernel,
        grid=(steps,),
        in_specs=[
            whole((slots + TAIL, width)), whole((slots + TAIL, width)),
            weights, weights, weights, weights,
        ]
        + [ANY] * len(ahead),
        out_specs=[
            out, out, out, out,
            whole((slots + TAIL, width)), whole((slots, width)),
            whole((width, slots)), whole((width, slots)),
        ],
        out_shape=[
            acts, acts, acts, acts,
            jax.ShapeDtypeStruct((slots + TAIL, width), BF16),
            jax.ShapeDtypeStruct((slots, width), BF16),
            jax.ShapeDtypeStruct((width, slots), BF16),
            jax.ShapeDtypeStruct((width, slots), BF16),
        ],
        scratch_shapes=[
            pltpu.VMEM((slots, width), BF16),
            pltpu.VMEM((slots, width), F32),
            pltpu.VMEM((slots, width), F32),
        ],
        compiler_params=pltpu.CompilerParams(vmem_limit_bytes=60 * MIB),
        cost_estimate=LIGHT,
        name="expert_chunk",
    )(rows, grads, own_in, own_out, other_in, other_out, *ahead)


def weight_grad_kernel(count, *refs):
    turned = refs[:count]
    acts = refs[count : 2 * count]
    out_ref = refs[-1]
    both_rows = jnp.concatenate([ref[...] for ref in turned], axis=1)
    both_acts = jnp.concatenate([ref[...] for ref in acts], axis=0)
    out_ref[...] = dot_nn(both_rows, both_acts).astype(BF16)


def weight_grad(turned, acts, ahead=()):
    count = len(turned)
    width, slots = turned[0].shape
    half = acts[0].shape[1]
    cols = 512
    return pl.pallas_call(
        functools.partial(weight_grad_kernel, count),
        grid=(half // cols,),
        in_specs=[whole((width, slots))] * count
        + [pl.BlockSpec((slots, cols), lambda f: (0, f))] * count
        + [ANY] * len(ahead),
        out_specs=pl.BlockSpec((width, cols), lambda f: (0, f)),
        out_shape=jax.ShapeDtypeStruct((width, half), BF16),
        compiler_params=pltpu.CompilerParams(vmem_limit_bytes=60 * MIB),
        cost_estimate=LIGHT,
        name="weight_grad",
    )(*turned, *acts, *ahead)


def combine_kernel(count, *refs):
    backs, ends = refs[:count], refs[count : 2 * count]
    (dest_ref, gates_ref, residual_ref, grad_ref, gain_ref, router_ref, w_ref) = refs[
        2 * count : 2 * count + 7
    ]
    (d_residual_ref, branch_ref, mixed_ref, gain_grad, logit_grad, stacked, tails) = refs[-7:]
    slots = backs[0].shape[0]

    @pl.when(pl.program_id(0) == 0)
    def _():
        gain_grad[...] = jnp.zeros_like(gain_grad)
        tails[...] = jnp.zeros_like(tails)
        for index, (back, end) in enumerate(zip(backs, ends)):
            columns = slice(index * slots, (index + 1) * slots)
            stacked[columns, :] = back[...]
            tails[index * TAIL : (index + 1) * TAIL, columns] = end[:, :slots]

    place = lax.broadcasted_iota(jnp.int32, (ROWS, slots), 1)
    lane = lax.broadcasted_iota(jnp.int32, (ROWS, 128), 1)
    dest = as_columns(dest_ref)
    hot = jnp.concatenate(
        [
            (place == dest[:, index : index + 1]).astype(F32).astype(BF16)
            for index in range(count)
        ],
        axis=1,
    )
    d_normed = dot_nn(hot, stacked[...])
    picked = dot_nt(hot, tails[...])
    d_gates = jnp.zeros((ROWS, 128), F32)
    for index in range(count):
        part = picked[:, index * TAIL : index * TAIL + 1]
        for extra in (1, 2):
            part = part + picked[:, index * TAIL + extra : index * TAIL + extra + 1]
        d_gates = jnp.where(lane == index, part, d_gates)
    gates = gates_ref[...]
    inner = jnp.sum(gates * d_gates, axis=1, keepdims=True)
    d_logits = gates * (d_gates - inner)
    logit_grad[...] = d_logits
    for index in range(count):
        d_normed = d_normed + d_logits[:, index : index + 1] * router_ref[index : index + 1, :]
    residual = residual_ref[...]
    scale = lax.rsqrt(jnp.mean(residual * residual, axis=1, keepdims=True) + EPS)
    unit = residual * scale
    scaled = gain_ref[...] * d_normed
    pull = jnp.mean(scaled * unit, axis=1, keepdims=True)
    d_residual = grad_ref[...].astype(F32) + scale * (scaled - unit * pull)
    d_residual_ref[...] = d_residual
    branch = d_residual.astype(BF16)
    branch_ref[...] = branch
    mixed_ref[...] = dot_nt(branch, w_ref[...]).astype(BF16)
    gain_grad[...] += jnp.sum(d_normed * unit, axis=0, keepdims=True)


def combine_back(backs, dest_row, gates, residual, grad, gain, router_rows, w_out, ahead=()):
    rows, width = residual.shape
    count = len(backs)
    slots = backs[0].shape[0] - TAIL
    block = lambda n: pl.BlockSpec((ROWS, n), lambda i: (i, 0))
    return pl.pallas_call(
        functools.partial(combine_kernel, count),
        grid=(rows // ROWS,),
        in_specs=[pl.BlockSpec((slots, width), lambda i: (0, 0))] * count
        + [pl.BlockSpec((TAIL, width), lambda i: (slots // TAIL, 0))] * count
        + [
            pl.BlockSpec((dest_row.shape[0], ROWS), lambda i: (0, i)),
            block(128), block(width), block(width), whole((1, width)),
            whole(router_rows.shape), whole((width, width)),
        ]
        + [ANY] * len(ahead),
        out_specs=[block(width), block(width), block(width), whole((1, width)), block(128)],
        out_shape=[
            jax.ShapeDtypeStruct((rows, width), F32),
            jax.ShapeDtypeStruct((rows, width), BF16),
            jax.ShapeDtypeStruct((rows, width), BF16),
            jax.ShapeDtypeStruct((1, width), F32),
            jax.ShapeDtypeStruct((rows, 128), F32),
        ],
        scratch_shapes=[
            pltpu.VMEM((count * slots, width), BF16),
            pltpu.VMEM((count * TAIL, count * slots), BF16),
        ],
        compiler_params=pltpu.CompilerParams(vmem_limit_bytes=60 * MIB),
        cost_estimate=LIGHT,
        name="combine_back",
    )(*backs, *backs, dest_row, gates, residual, grad, gain, router_rows, w_out, *ahead)


def output_kernel(count, *refs):
    mades = refs[:count]
    dest_ref, gates_ref, residual_ref = refs[count : count + 3]
    out_ref = refs[-1]
    slots = mades[0].shape[0]
    place = lax.broadcasted_iota(jnp.int32, (ROWS, slots), 1)
    dest = as_columns(dest_ref)
    total = residual_ref[...]
    for index, made in enumerate(mades):
        hot = (place == dest[:, index : index + 1]).astype(F32).astype(BF16)
        total = total + gates_ref[:, index : index + 1] * dot_nn(hot, made[...])
    out_ref[...] = total.astype(BF16)


def combine_output(mades, dest_row, gates, residual, ahead=()):
    rows, width = residual.shape
    count = len(mades)
    slots = mades[0].shape[0]
    block = lambda n: pl.BlockSpec((ROWS, n), lambda i: (i, 0))
    return pl.pallas_call(
        functools.partial(output_kernel, count),
        grid=(rows // ROWS,),
        in_specs=[pl.BlockSpec((slots, width), lambda i: (0, 0))] * count
        + [pl.BlockSpec((dest_row.shape[0], ROWS), lambda i: (0, i)), block(128), block(width)]
        + [ANY] * len(ahead),
        out_specs=block(width),
        out_shape=jax.ShapeDtypeStruct((rows, width), BF16),
        compiler_params=pltpu.CompilerParams(vmem_limit_bytes=60 * MIB),
        cost_estimate=LIGHT,
        name="combine_output",
    )(*mades, dest_row, gates, residual, *ahead)


def final_kernel(dqkv_ref, w_ref, tokens_ref, gain_ref, d_residual_ref, *rest):
    out_ref = rest[-1]
    width = tokens_ref.shape[1]
    d_normed = (
        dot_nt(dqkv_ref[0], w_ref[:, :width])
        + dot_nt(dqkv_ref[1], w_ref[:, width : 2 * width])
        + dot_nt(dqkv_ref[2], w_ref[:, 2 * width : 3 * width])
    )
    tokens = tokens_ref[...].astype(F32)
    scale = lax.rsqrt(jnp.mean(tokens * tokens, axis=1, keepdims=True) + EPS)
    unit = tokens * scale
    scaled = gain_ref[...] * d_normed
    pull = jnp.mean(scaled * unit, axis=1, keepdims=True)
    out_ref[...] = d_residual_ref[...] + scale * (scaled - unit * pull)


def final_tokens(d_qkv, w_all, tokens, gain, d_residual, ahead=()):
    rows, width = tokens.shape
    block = lambda n: pl.BlockSpec((ROWS, n), lambda i: (i, 0))
    return pl.pallas_call(
        final_kernel,
        grid=(rows // ROWS,),
        in_specs=[
            pl.BlockSpec((3, ROWS, width), lambda i: (0, i, 0)), whole((width, 3 * width)),
            block(width), whole((1, width)), block(width),
        ]
        + [ANY] * len(ahead),
        out_specs=block(width),
        out_shape=jax.ShapeDtypeStruct((rows, width), F32),
        compiler_params=pltpu.CompilerParams(vmem_limit_bytes=60 * MIB),
        cost_estimate=LIGHT,
        name="final_tokens",
    )(d_qkv, w_all, tokens, gain, d_residual, *ahead)


def qkv_grad_kernel(parts, turned_ref, grad_ref, mixed_ref, branch_ref, extra_ref, *rest):
    step = pl.program_id(0)
    keep_ref, send_ref = rest[-2:]
    half = keep_ref.shape[0]

    def store(made):
        keep_ref[...] = made[:half]
        send_ref[...] = made[half:]

    @pl.when(step < 3 * parts)
    def _():
        store(dot_nn(turned_ref[...], grad_ref[0]).astype(BF16))

    @pl.when((step >= 3 * parts) & (step < 4 * parts))
    def _():
        store(dot_nn(mixed_ref[...], branch_ref[...]).astype(BF16))

    @pl.when(step == 4 * parts)
    def _():
        store(extra_ref[...])


def qkv_grad(turned, d_qkv, mixed_turned, branch, extra, ahead=()):
    width, rows = turned.shape
    parts = width // BLK

    def place(j):
        j = jnp.minimum(j, 3 * parts - 1)
        return (j // parts, 0, j % parts)

    def place_branch(j):
        return (0, jnp.clip(j - 3 * parts, 0, parts - 1))

    return pl.pallas_call(
        functools.partial(qkv_grad_kernel, parts),
        grid=(4 * parts + 1,),
        in_specs=[
            whole((width, rows)), pl.BlockSpec((1, rows, BLK), place),
            whole((width, rows)), pl.BlockSpec((rows, BLK), place_branch), whole((width, BLK)),
        ]
        + [ANY] * len(ahead),
        out_specs=[pl.BlockSpec((width // 2, BLK), lambda j: (0, j))] * 2,
        out_shape=[jax.ShapeDtypeStruct((width // 2, 4 * width + BLK), BF16)] * 2,
        compiler_params=pltpu.CompilerParams(vmem_limit_bytes=60 * MIB),
        cost_estimate=LIGHT,
        name="qkv_grad",
    )(turned, d_qkv, mixed_turned, branch, extra, *ahead)


def pairs_of(size, offset):
    return [(i, i ^ offset) for i in range(size)]


def gather_line(block):
    dp_size = lax.axis_size("dp")
    line = [block]
    for m in range(1, dp_size):
        line.append(lax.ppermute(block, "dp", pairs_of(dp_size, m)))
    return jnp.concatenate(line, axis=0)


def gather_plane(line, ahead):
    fsdp_size = lax.axis_size("fsdp")
    plane = [line]
    for m in range(1, fsdp_size // 2):
        plane.append(lax.ppermute(line, "fsdp", pairs_of(fsdp_size, 2 * m)))
    (plane,) = held([jnp.concatenate(plane, axis=0)], ahead)
    other = lax.ppermute(plane, "fsdp", pairs_of(fsdp_size, 1))
    return plane, other, jnp.concatenate([plane, other], axis=0)


def scatter_pair(keep, send):
    fsdp_size = lax.axis_size("fsdp")
    got = lax.ppermute(send, "fsdp", pairs_of(fsdp_size, 1))
    return (keep.astype(F32) + got.astype(F32)).astype(BF16)


def scatter_plane(plane):
    fsdp_size = lax.axis_size("fsdp")
    rows = 2 * plane.shape[0] // fsdp_size
    line = plane[:rows].astype(F32)
    for m in range(1, fsdp_size // 2):
        got = lax.ppermute(plane[m * rows : (m + 1) * rows], "fsdp", pairs_of(fsdp_size, 2 * m))
        line = line + got.astype(F32)
    return line.astype(BF16)


def scatter_line(line):
    dp_size = lax.axis_size("dp")
    rows = line.shape[0] // dp_size
    total = line[:rows].astype(F32)
    for m in range(1, dp_size):
        got = lax.ppermute(line[m * rows : (m + 1) * rows], "dp", pairs_of(dp_size, m))
        total = total + got.astype(F32)
    return total


def position_matrix(width):
    dp_size, fsdp_size = lax.axis_size("dp"), lax.axis_size("fsdp")
    layer, place = lax.axis_index("dp"), lax.axis_index("fsdp")
    chips = fsdp_size // 2
    rows = width // (dp_size * fsdp_size)
    position = jnp.arange(width, dtype=jnp.int32)
    row = position % rows
    layer_of = (position // rows) % dp_size ^ layer
    chip_of = (position // (rows * dp_size)) % chips ^ (place // 2)
    core_of = position // (rows * dp_size * chips) ^ (place % 2)
    source = ((layer_of * chips + chip_of) * 2 + core_of) * rows + row
    return (position[:, None] == source[None, :]).astype(BF16)


def local(
    tokens_in, w_qkv, w_attn_out, gain_attn, gain_ffn, rel_bias, router, w_in, w_out,
    segment_ids, expert_ids, d_out,
):
    tok_rows, width = tokens_in.shape
    top_count = expert_ids.shape[1]
    fsdp_size = lax.axis_size("fsdp")
    experts = fsdp_size // 2
    slots = min(tok_rows, tok_rows * top_count * 5 // (4 * experts))
    me = lax.axis_index("fsdp") // 2

    own_in = lax.all_gather(w_in, "dp", axis=0, tiled=True)
    own_out = lax.all_gather(w_out, "dp", axis=0, tiled=True)
    small = jnp.concatenate(
        [router, gain_attn[:, None], gain_ffn[:, None], rel_bias[:, None]], axis=1
    )
    small = jnp.pad(small, ((0, 0), (0, 128 - small.shape[1])))
    relative = expert_ids ^ me
    hot = jnp.sum(
        (relative[:, :, None] == jnp.arange(experts, dtype=jnp.int32)).astype(jnp.int32), axis=1
    )
    rank = jnp.cumsum(hot, axis=0) - hot
    dest = jnp.where(hot > 0, rank, -1)
    lines = max(8, experts)
    dest_row = jnp.pad(dest.T, ((0, lines - experts), (0, 0)), constant_values=-1)

    def exchange(pieces):
        return [pieces[0]] + [
            lax.ppermute(pieces[m], "fsdp", pairs_of(fsdp_size, 2 * m)) for m in range(1, experts)
        ]

    line = gather_line(jnp.concatenate([w_qkv, w_attn_out, small], axis=1))
    sent_grads = dispatch(
        experts, dest_row, d_out, jnp.zeros((lines, tok_rows), F32), slots, (line,)
    )
    move = position_matrix(width)
    (tokens_after,) = held([tokens_in], (line,))
    tokens = tokens_after.astype(F32)
    scale = lax.rsqrt(jnp.mean(tokens * tokens, axis=1, keepdims=True) + EPS)
    unit = jnp.dot(tokens_after, move, preferred_element_type=F32) * scale
    plane, plane_rest, full = gather_plane(line, (sent_grads[1], unit))
    grads_in = exchange([sent_grads[0]] + list(held(sent_grads[1:], (plane,))))

    moved_gain = full[:, 4 * width + experts].astype(F32).reshape(1, width)
    columns = jnp.dot(move, full[:, 4 * width :], preferred_element_type=F32).astype(BF16)
    back_qkv = jnp.dot(move, full[:, : 3 * width], preferred_element_type=F32).astype(BF16)
    back_attn = jnp.dot(
        move, full[:, 3 * width : 4 * width], preferred_element_type=F32
    ).astype(BF16)
    by_row = columns.T
    gain_a = by_row[experts : experts + 1].astype(F32)
    gain_f = by_row[experts + 1 : experts + 2].astype(F32)
    table = by_row[experts + 2].reshape(HEADS, BUCKETS)
    bucket_hot = (
        buckets_of(jnp.arange(BLK, dtype=jnp.int32))[:, None]
        == jnp.arange(BUCKETS, dtype=jnp.int32)[None, :]
    )
    near = jnp.dot(table, bucket_hot.T.astype(BF16), preferred_element_type=F32)
    near = near.reshape(HEADS // 2, 2, BLK)
    far = table[:, BUCKETS - 1].astype(F32)
    place = jnp.arange(128, dtype=jnp.int32)
    swap = ((place[:, None] ^ me) == place[None, :]) & (place[:, None] < experts)
    router_cols = jnp.dot(columns, swap.astype(BF16), preferred_element_type=F32).astype(BF16)
    router_rows = router_cols.T[: max(8, experts)].astype(F32)

    normed_attn = (unit * moved_gain).astype(BF16)
    qkv_rows = jnp.dot(normed_attn, full[:, : 3 * width], preferred_element_type=F32).astype(BF16)
    segments = segment_ids.reshape(tok_rows)
    mixed, lse = attention_forward(qkv_rows, segments, near, far, HEADS)
    residual, normed_ffn, gates, gate_row, moved_mixed = post_attention(
        mixed, plane, plane_rest, tokens_in, gain_f, router_cols, dest_row, move,
        tuple(grads_in[1:3]),
    )
    sent_rows = dispatch(experts, dest_row, normed_ffn, gate_row, slots, tuple(grads_in[3:]))
    rows_in = exchange(sent_rows)
    (own_in,) = held([own_in], (mixed,))
    (own_out,) = held([own_out], (sent_rows[0],))
    other_in = lax.ppermute(own_in, "fsdp", pairs_of(fsdp_size, 1))
    other_out = lax.ppermute(own_out, "fsdp", pairs_of(fsdp_size, 1))

    chunks, backs = [], []
    for m in range(experts):
        ahead = tuple(backs[1 : m - 1]) + ((chunks[-1][4],) if chunks else ())
        chunks.append(
            expert_chunk(rows_in[m], grads_in[m], own_in, own_out, other_in, other_out, ahead)
        )
        back = chunks[-1][4]
        backs.append(
            lax.ppermute(back, "fsdp", pairs_of(fsdp_size, 2 * m)) if m > 0 else back
        )
    hid_own, hid_other, dpre_own, dpre_other, _, made, rows_turned, gexp_turned = zip(*chunks)

    def pair_sum(own, other):
        got = lax.ppermute(other, "fsdp", pairs_of(fsdp_size, 1))
        return (own.astype(F32) + got.astype(F32)).astype(BF16)

    def owners(pair):
        return lax.psum_scatter(pair, "dp", scatter_dimension=0, tiled=True).astype(F32)

    grad_in_own = weight_grad(rows_turned, dpre_own, tuple(backs[-2:-1]))
    grad_out_own = weight_grad(gexp_turned, hid_own, (grad_in_own,))
    grad_in_other = weight_grad(rows_turned, dpre_other, (grad_out_own,) + tuple(backs[-1:]))
    pair_in = pair_sum(grad_in_own, grad_in_other)
    grad_out_other = weight_grad(gexp_turned, hid_other, (pair_in,))
    pair_out = pair_sum(grad_out_own, grad_out_other)
    d_w_in, d_w_out = owners(pair_in), owners(pair_out)
    mades = exchange([made[0]] + list(held(made[1:], (pair_out,))))

    d_residual, d_branch, d_mixed, d_gain_f, d_logits = combine_back(
        backs, dest_row, gates, residual, d_out, gain_f, router_rows, back_attn, (grad_out_other, pair_in, pair_out)
    )
    d_qkv, near_grad, far_grad = attention_backward(
        qkv_rows, d_mixed, mixed, lse, segments, near, far, HEADS
    )
    near_grad, far_grad = held([near_grad, far_grad], tuple(mades[1:]))
    d_router = jnp.dot(normed_ffn.T, d_logits.astype(BF16), preferred_element_type=F32)
    d_router = jnp.dot(d_router, swap.T.astype(F32), precision=lax.Precision.HIGHEST)
    d_table = jnp.dot(
        near_grad.reshape(HEADS, BLK), bucket_hot.astype(F32), precision=lax.Precision.HIGHEST
    )
    last = jnp.arange(BUCKETS, dtype=jnp.int32)[None, :] == BUCKETS - 1
    d_table = d_table + jnp.where(last, far_grad[:, :, :1].reshape(HEADS, 1), 0.0)
    late_cols = jnp.where(place[None, :] == experts, d_gain_f.reshape(width, 1), d_router)
    late_cols = jnp.where(place[None, :] == experts + 1, d_table.reshape(width, 1), late_cols)
    late_cols = jnp.dot(move.T, late_cols.astype(BF16), preferred_element_type=F32)
    late_cols = jnp.pad(late_cols.astype(BF16), ((0, 0), (0, BLK - 128)))
    keep, send = qkv_grad(
        normed_attn.T, d_qkv, moved_mixed.T, d_branch, late_cols, (d_w_in,)
    )
    keep, send = held([keep, send], (d_w_out,))
    late = scatter_plane(scatter_pair(keep, send))
    block_out = combine_output(mades, dest_row, gates, residual)
    d_tokens = final_tokens(d_qkv, back_qkv, tokens_in, gain_a, d_residual, (block_out,))
    (late,) = held([late], (d_tokens,))
    late = scatter_line(late)
    own_qkv = late[:, : 3 * width]
    own_gain_a = jnp.sum(own_qkv * w_qkv.astype(F32), axis=1) / gain_attn.astype(F32)
    return (
        block_out,
        d_tokens,
        own_qkv,
        late[:, 3 * width : 4 * width],
        own_gain_a,
        late[:, 4 * width + experts],
        late[:, 4 * width + experts + 1],
        late[:, 4 * width : 4 * width + experts],
        d_w_in,
        d_w_out,
    )


def solution(mesh):
    both = P(("dp", "fsdp"), None)
    line = P(("dp", "fsdp"))
    tiles = P("dp", "fsdp")
    return jax.shard_map(
        local,
        mesh=mesh,
        in_specs=(both, both, both, line, line, line, both, tiles, tiles, both, both, both),
        out_specs=(both, both, both, both, line, line, line, both, tiles, tiles),
        check_vma=False,
    )
```

```python
import functools
import math

import jax
import jax.numpy as jnp
from jax import lax
from jax.experimental import pallas as pl
from jax.experimental.pallas import tpu as pltpu
from jax.sharding import PartitionSpec as P

NEG = -1e30
BLK = 256
SPAN = 2
F32 = jnp.float32
BF16 = jnp.bfloat16
LIGHT = pl.CostEstimate(flops=1000, bytes_accessed=1000, transcendentals=0)


def dot_nt(a, b):
    return lax.dot_general(a, b, (((1,), (1,)), ((), ())), preferred_element_type=F32)


def dot_nn(a, b):
    return lax.dot_general(a, b, (((1,), (0,)), ((), ())), preferred_element_type=F32)


def fill_masks(mask, seg_row, seg_col, blocks):
    key_place = lax.broadcasted_iota(jnp.int32, (BLK, BLK), 0)
    row_place = lax.broadcasted_iota(jnp.int32, (BLK, BLK), 1)
    for kb in range(blocks):
        keys = seg_col[kb * BLK : (kb + 1) * BLK, :]
        for step in range(min(SPAN + 1, blocks - kb)):
            rows = seg_row[:, (kb + step) * BLK : (kb + step + 1) * BLK]
            seen = keys == rows
            if step == 0:
                seen = seen & (row_place >= key_place)
            mask[kb, step] = jnp.where(seen, 0.0, NEG)


def bias_tiles(near_row, far_value):
    key_place = lax.broadcasted_iota(jnp.int32, (BLK, BLK), 0)
    row_place = lax.broadcasted_iota(jnp.int32, (BLK, BLK), 1)
    rolled = pltpu.roll(
        jnp.broadcast_to(near_row, (BLK, BLK)), 0, 1, stride=1, stride_axis=0
    )
    return rolled, jnp.where(row_place < key_place, rolled, far_value)


def head_lanes(values, half):
    lane = lax.broadcasted_iota(jnp.int32, values.shape, 1)
    keep = (lane >= 64) if half else (lane < 64)
    return jnp.where(keep, values, jnp.zeros_like(values))


def attn_fwd_kernel(
    far_ref, q_ref, k_ref, v_ref, near_ref, seg_row, seg_col, *rest
):
    o_ref, lse_ref, mask, turned = rest[-4:]
    pair = pl.program_id(0)
    length = q_ref.shape[0]
    blocks = length // BLK

    @pl.when(pair == 0)
    def _():
        fill_masks(mask, seg_row, seg_col, blocks)

    v_turned = v_ref[...].T
    ones = jnp.ones((16, length), BF16)
    for half in range(2):
        far_value = far_ref[pair * 2 + half]
        diag, below = bias_tiles(near_ref[0, half : half + 1, :], far_value)
        keys = head_lanes(k_ref[...], half)
        values = jnp.concatenate([v_turned[64 * half : 64 * half + 64], ones], axis=0)
        for a in range(blocks):
            first = max(0, a - SPAN)
            q_rows = q_ref[a * BLK : (a + 1) * BLK, :] * jnp.asarray(0.125, BF16)
            parts = []
            for kb in range(first, a + 1):
                part = dot_nt(keys[kb * BLK : (kb + 1) * BLK], q_rows)
                bias = (diag, below, far_value)[a - kb]
                parts.append(part + bias + mask[kb, a - kb])
            peak = functools.reduce(
                jnp.maximum, [jnp.max(part, axis=0, keepdims=True) for part in parts]
            )
            weights = jnp.concatenate(
                [jnp.exp(part - peak).astype(BF16) for part in parts], axis=0
            )
            made = dot_nn(values[:, first * BLK : (a + 1) * BLK], weights)
            total = made[64:65]
            turned[64 * half : 64 * half + 64, a * BLK : (a + 1) * BLK] = made[:64] / total
            lse_ref[0, half : half + 1, a * BLK : (a + 1) * BLK] = peak + jnp.log(total)
    o_ref[...] = turned[...].T.astype(BF16)


def attn_bwd_kernel(
    far_ref, q_ref, k_ref, v_ref, g_ref, o_ref, lse_ref, near_ref, seg_row, seg_col, *rest
):
    d_ref, near_grad, far_grad, mask, turned = rest[-5:]
    pair = pl.program_id(0)
    length = q_ref.shape[0]
    blocks = length // BLK

    @pl.when(pair == 0)
    def _():
        fill_masks(mask, seg_row, seg_col, blocks)

    scaled = q_ref[...] * jnp.asarray(0.125, BF16)
    k_turned = k_ref[...].T
    ones = jnp.ones((16, length), BF16)
    inner = (g_ref[...].astype(F32) * o_ref[...].astype(F32)).T
    key_place = lax.broadcasted_iota(jnp.int32, (BLK, BLK), 0)
    row_place = lax.broadcasted_iota(jnp.int32, (BLK, BLK), 1)
    key_grads = [None] * blocks
    value_grads = [None] * blocks
    for half in range(2):
        far_value = far_ref[pair * 2 + half]
        diag, below = bias_tiles(near_ref[0, half : half + 1, :], far_value)
        keys = head_lanes(k_ref[...], half)
        values = head_lanes(v_ref[...], half)
        q_own = head_lanes(scaled, half)
        g_own = head_lanes(g_ref[...], half)
        keys_turned = jnp.concatenate([k_turned[64 * half : 64 * half + 64], ones], axis=0)
        delta = jnp.sum(inner[64 * half : 64 * half + 64], axis=0, keepdims=True)
        lse = lse_ref[0, half : half + 1, :]
        diag_grad = jnp.zeros((BLK, BLK), F32)
        below_grad = jnp.zeros((BLK, BLK), F32)
        turned[...] = jnp.zeros_like(turned)
        for kb in range(blocks):
            last = min(kb + SPAN + 1, blocks)
            k_rows = keys[kb * BLK : (kb + 1) * BLK]
            v_rows = values[kb * BLK : (kb + 1) * BLK]
            probs, grads = [], []
            for a in range(kb, last):
                rows = slice(a * BLK, (a + 1) * BLK)
                score = dot_nt(k_rows, scaled[rows])
                d_prob = dot_nt(v_rows, g_ref[rows, :])
                bias = (diag, below, far_value)[a - kb]
                prob = jnp.exp(score + bias + mask[kb, a - kb] - lse[:, rows])
                d_score = prob * (d_prob - delta[:, rows])
                if a == kb:
                    diag_grad = diag_grad + d_score
                elif a == kb + 1:
                    below_grad = below_grad + d_score
                probs.append(prob.astype(BF16))
                grads.append(d_score.astype(BF16))
            wide = slice(kb * BLK, last * BLK)
            prob_wide = jnp.concatenate(probs, axis=1)
            grad_wide = jnp.concatenate(grads, axis=1)
            value_grad = dot_nn(prob_wide, g_own[wide])
            key_grad = dot_nn(grad_wide, q_own[wide])
            turned[:, wide] += dot_nn(keys_turned[:, kb * BLK : (kb + 1) * BLK], grad_wide)
            if half == 0:
                value_grads[kb], key_grads[kb] = value_grad, key_grad
            else:
                rows = slice(kb * BLK, (kb + 1) * BLK)
                d_ref[2, rows, :] = (value_grads[kb] + value_grad).astype(BF16)
                d_ref[1, rows, :] = (key_grads[kb] + key_grad).astype(BF16)
        part = (turned[:64] * 0.125).T
        if half == 0:
            first_part = part
        else:
            d_ref[0] = jnp.concatenate([first_part, part], axis=1).astype(BF16)
        by_offset = diag_grad + jnp.where(row_place < key_place, below_grad, 0.0)
        for bit in range(8):
            by_offset = jnp.where(
                ((key_place >> bit) & 1) == 1,
                pltpu.roll(by_offset, BLK - (1 << bit), 1),
                by_offset,
            )
        near = jnp.sum(by_offset, axis=0, keepdims=True)
        near_grad[0, half : half + 1, :] = near
        everything = jnp.sum(turned[64:65, :], axis=1, keepdims=True)
        rest = everything - jnp.sum(near, axis=1, keepdims=True)
        far_grad[0, half : half + 1, :] = jnp.broadcast_to(rest, (1, 128))


def attention_specs(length, pairs):
    def column(offset):
        return pl.BlockSpec((length, 128), lambda p, far: (0, p + offset))

    return column


def attention_forward(qkv_rows, segments, near, far, heads, ahead=()):
    length = qkv_rows.shape[0]
    pairs = heads // 2
    width = heads * 64
    column = attention_specs(length, pairs)
    blocks = length // BLK
    return pl.pallas_call(
        attn_fwd_kernel,
        grid_spec=pltpu.PrefetchScalarGridSpec(
            num_scalar_prefetch=1,
            grid=(pairs,),
            in_specs=[
                column(0),
                column(pairs),
                column(2 * pairs),
                pl.BlockSpec((1, 2, BLK), lambda p, far: (p, 0, 0)),
                pl.BlockSpec((1, length), lambda p, far: (0, 0)),
                pl.BlockSpec((length, 1), lambda p, far: (0, 0)),
            ]
            + [pl.BlockSpec(memory_space=pl.ANY)] * len(ahead),
            out_specs=[
                column(0),
                pl.BlockSpec((1, 2, length), lambda p, far: (p, 0, 0)),
            ],
            scratch_shapes=[
                pltpu.VMEM((blocks, SPAN + 1, BLK, BLK), F32),
                pltpu.VMEM((128, length), F32),
            ],
        ),
        out_shape=[
            jax.ShapeDtypeStruct((length, width), BF16),
            jax.ShapeDtypeStruct((pairs, 2, length), F32),
        ],
        compiler_params=pltpu.CompilerParams(vmem_limit_bytes=60 * 1024 * 1024),
        cost_estimate=LIGHT,
        name="attention_forward",
    )(far, qkv_rows, qkv_rows, qkv_rows, near, segments.reshape(1, length), segments.reshape(length, 1), *ahead)


def attention_backward(qkv_rows, d_mixed, mixed, lse, segments, near, far, heads, ahead=()):
    length = qkv_rows.shape[0]
    pairs = heads // 2
    width = heads * 64
    column = attention_specs(length, pairs)
    blocks = length // BLK
    small = lambda n: pl.BlockSpec((1, 2, n), lambda p, far: (p, 0, 0))
    return pl.pallas_call(
        attn_bwd_kernel,
        grid_spec=pltpu.PrefetchScalarGridSpec(
            num_scalar_prefetch=1,
            grid=(pairs,),
            in_specs=[
                column(0),
                column(pairs),
                column(2 * pairs),
                column(0),
                column(0),
                small(length),
                small(BLK),
                pl.BlockSpec((1, length), lambda p, far: (0, 0)),
                pl.BlockSpec((length, 1), lambda p, far: (0, 0)),
            ]
            + [pl.BlockSpec(memory_space=pl.ANY)] * len(ahead),
            out_specs=[
                pl.BlockSpec((3, length, 128), lambda p, far: (0, 0, p)),
                small(BLK),
                small(128),
            ],
            scratch_shapes=[
                pltpu.VMEM((blocks, SPAN + 1, BLK, BLK), F32),
                pltpu.VMEM((80, length), F32),
            ],
        ),
        out_shape=[
            jax.ShapeDtypeStruct((3, length, width), BF16),
            jax.ShapeDtypeStruct((pairs, 2, BLK), F32),
            jax.ShapeDtypeStruct((pairs, 2, 128), F32),
        ],
        compiler_params=pltpu.CompilerParams(vmem_limit_bytes=60 * 1024 * 1024),
        cost_estimate=LIGHT,
        name="attention_backward",
    )(
        far, qkv_rows, qkv_rows, qkv_rows, d_mixed, mixed, lse, near,
        segments.reshape(1, length), segments.reshape(length, 1), *ahead,
    )


HEADS = 12
BUCKETS = 64
MAX_DIST = 128
EPS = 1e-06
ROWS = 256
TAIL = 16
COEF = math.sqrt(2.0 / math.pi)
CUBIC = 0.044715
MIB = 1024 * 1024


def bucket_bounds(bucket_count, max_distance):
    halfway = bucket_count // 2
    bounds = []
    for bucket in range(bucket_count):
        if bucket < halfway:
            bounds.append(bucket)
        else:
            bounds.append(
                int(math.ceil(halfway * (max_distance / halfway) ** ((bucket - halfway) / halfway)))
            )
    return bounds


def buckets_of(distance):
    limits = jnp.array(bucket_bounds(BUCKETS, MAX_DIST), dtype=jnp.int32)
    reached = (distance[:, None] >= limits[None, :]).astype(jnp.int32)
    return jnp.sum(reached, axis=1) - 1


def whole(shape):
    return pl.BlockSpec(shape, lambda *_: (0,) * len(shape))


def split_three(values):
    high = values.astype(BF16)
    rest = values - high.astype(F32)
    middle = rest.astype(BF16)
    low = (rest - middle.astype(F32)).astype(BF16)
    return high, middle, low


ANY = pl.BlockSpec(memory_space=pl.ANY)


def dispatch_kernel(experts, dest_ref, values_ref, gate_ref, *rest):
    out_refs = rest[-experts:]
    slots = out_refs[0].shape[0] - TAIL
    tokens = values_ref.shape[0]
    own = pl.ds(pl.program_id(0), 1)
    place = lax.broadcasted_iota(jnp.int32, (slots, tokens), 0)
    hot = (place == dest_ref[own, :]).astype(F32).astype(BF16)
    rows = dot_nn(hot, values_ref[...]).astype(BF16)
    pieces = split_three(jnp.broadcast_to(gate_ref[own, :], (TAIL, tokens)))
    line = lax.broadcasted_iota(jnp.int32, (TAIL, tokens), 0)
    stacked = jnp.zeros((TAIL, tokens), F32)
    for index, piece in enumerate(pieces):
        stacked = jnp.where(line == index, piece.astype(F32), stacked)
    tail = dot_nt(stacked.astype(BF16), hot).astype(BF16)
    for index, out_ref in enumerate(out_refs):

        @pl.when(pl.program_id(0) == index)
        def _():
            out_ref[:slots, :] = rows
            out_ref[slots:, :] = jnp.zeros((TAIL, out_ref.shape[1]), BF16)
            out_ref[slots:, :slots] = tail


def dispatch(experts, dest_row, values, gate_row, slots, ahead=()):
    tokens, width = values.shape
    return pl.pallas_call(
        functools.partial(dispatch_kernel, experts),
        grid=(experts,),
        in_specs=[
            whole(dest_row.shape), whole((tokens, width)), whole(gate_row.shape),
        ]
        + [ANY] * len(ahead),
        out_specs=[whole((slots + TAIL, width))] * experts,
        out_shape=[jax.ShapeDtypeStruct((slots + TAIL, width), BF16)] * experts,
        compiler_params=pltpu.CompilerParams(vmem_limit_bytes=60 * MIB),
        cost_estimate=LIGHT,
        name="dispatch_rows",
    )(dest_row, values, gate_row, *ahead)


def nothing_kernel(*refs):
    pass


def held(values, ahead):
    count = len(values)
    return pl.pallas_call(
        nothing_kernel,
        in_specs=[ANY] * (count + len(ahead)),
        out_specs=[ANY] * count,
        out_shape=[jax.ShapeDtypeStruct(value.shape, value.dtype) for value in values],
        input_output_aliases={index: index for index in range(count)},
        cost_estimate=LIGHT,
        name="held",
    )(*values, *ahead)


def as_columns(ref):
    rows = ref[...].astype(F32)
    filler = jnp.full((128 - rows.shape[0], rows.shape[1]), -1.0, F32)
    return jnp.concatenate([rows, filler], axis=0).T.astype(jnp.int32)


def post_kernel(
    mixed_ref, w_ref, w_rest, tokens_ref, gain_ref, router_ref, dest_ref, move_ref, *rest
):
    residual_ref, normed_ref, gates_ref, turned_ref, moved_ref = rest[-5:]
    half = w_ref.shape[0]
    moved = dot_nn(mixed_ref[...], move_ref[...]).astype(BF16)
    moved_ref[...] = moved
    residual = dot_nn(moved[:, :half], w_ref[...]) + dot_nn(moved[:, half:], w_rest[...])
    residual = tokens_ref[...].astype(F32) + residual
    residual_ref[...] = residual
    scale = lax.rsqrt(jnp.mean(residual * residual, axis=1, keepdims=True) + EPS)
    normed = (residual * scale * gain_ref[...]).astype(BF16)
    normed_ref[...] = normed
    logits = dot_nn(normed, router_ref[...])
    chosen = as_columns(dest_ref) >= 0
    logits = jnp.where(chosen, logits, NEG)
    peak = jnp.max(logits, axis=1, keepdims=True)
    weights = jnp.where(chosen, jnp.exp(logits - peak), 0.0)
    gates = weights / jnp.sum(weights, axis=1, keepdims=True)
    gates_ref[...] = gates
    turned_ref[...] = gates.T[: turned_ref.shape[0]]


def post_attention(mixed, w_top, w_rest, tokens, gain, router, dest_row, move, ahead=()):
    rows, width = tokens.shape
    lines = dest_row.shape[0]
    block = lambda n: pl.BlockSpec((ROWS, n), lambda i: (i, 0))
    return pl.pallas_call(
        post_kernel,
        grid=(rows // ROWS,),
        in_specs=[
            block(width), pl.BlockSpec((width // 2, width), lambda i: (0, 3)),
            pl.BlockSpec((width // 2, width), lambda i: (0, 3)), block(width),
            whole((1, width)), whole((width, 128)),
            pl.BlockSpec((lines, ROWS), lambda i: (0, i)), whole((width, width)),
        ]
        + [ANY] * len(ahead),
        out_specs=[
            block(width), block(width), block(128),
            pl.BlockSpec((lines, ROWS), lambda i: (0, i)), block(width),
        ],
        out_shape=[
            jax.ShapeDtypeStruct((rows, width), F32),
            jax.ShapeDtypeStruct((rows, width), BF16),
            jax.ShapeDtypeStruct((rows, 128), F32),
            jax.ShapeDtypeStruct((lines, rows), F32),
            jax.ShapeDtypeStruct((rows, width), BF16),
        ],
        compiler_params=pltpu.CompilerParams(vmem_limit_bytes=60 * MIB),
        cost_estimate=LIGHT,
        name="post_attention",
    )(mixed, w_top, w_rest, tokens, gain, router, dest_row, move, *ahead)


def expert_kernel(
    rows_ref, grads_ref, in_own, out_own, in_other, out_other, *rest
):
    hid_own, hid_other, dpre_own, dpre_other, back_ref, made_ref = rest[-11:-5]
    rows_turned, gexp_turned, gexp, made_sum, back_sum = rest[-5:]
    step = pl.program_id(0)
    slots = gexp.shape[0]

    @pl.when(step == 0)
    def _():
        turned = rows_ref[slots:, :slots].astype(F32).T
        gate = jnp.sum(turned, axis=1, keepdims=True)
        gexp[...] = (grads_ref[:slots, :].astype(F32) * gate).astype(BF16)
        gexp_turned[...] = gexp[...].T
        rows_turned[...] = rows_ref[:slots, :].T
        made_sum[...] = jnp.zeros_like(made_sum)
        back_sum[...] = jnp.zeros_like(back_sum)

    rows = rows_ref[:slots, :]
    hiddens, d_pres = [], []
    for w_in, w_out, hid, dpre in (
        (in_own, out_own, hid_own, dpre_own),
        (in_other, out_other, hid_other, dpre_other),
    ):
        pre = dot_nn(rows, w_in[...])
        d_hidden = dot_nn(gexp[...], w_out[...])
        square = pre * pre
        half = 0.5 + 0.5 * jnp.tanh(pre * (COEF + COEF * CUBIC * square))
        hidden = pre * half
        slope = half + hidden * (1.0 - half) * (2.0 * COEF + 6.0 * COEF * CUBIC * square)
        hidden_low = hidden.astype(BF16)
        d_pre = (d_hidden * slope).astype(BF16)
        hid[...] = hidden_low
        dpre[...] = d_pre
        hiddens.append(hidden_low)
        d_pres.append(d_pre)
    both_out = jnp.concatenate([out_own[...], out_other[...]], axis=1)
    both_in = jnp.concatenate([in_own[...], in_other[...]], axis=1)
    made_sum[...] += dot_nt(jnp.concatenate(hiddens, axis=1), both_out)
    back_sum[...] += dot_nt(jnp.concatenate(d_pres, axis=1), both_in)

    @pl.when(step == pl.num_programs(0) - 1)
    def _():
        made = made_sum[...]
        made_ref[...] = made.astype(BF16)
        back_ref[:slots, :] = back_sum[...].astype(BF16)
        by_gate = jnp.sum(grads_ref[:slots, :].astype(F32) * made, axis=1, keepdims=True)
        pieces = split_three(jnp.broadcast_to(by_gate, (slots, 128)))
        lane = lax.broadcasted_iota(jnp.int32, (slots, 128), 1)
        stacked = jnp.zeros((slots, 128), F32)
        for index, piece in enumerate(pieces):
            stacked = jnp.where(lane == index, piece.astype(F32), stacked)
        back_ref[slots:, :] = jnp.zeros((TAIL, back_ref.shape[1]), BF16)
        back_ref[slots:, :slots] = stacked.T[:TAIL].astype(BF16)


def expert_chunk(rows, grads, own_in, own_out, other_in, other_out, ahead=()):
    slots, width = rows.shape[0] - TAIL, rows.shape[1]
    half = own_in.shape[1]
    cols = 256
    steps = half // cols
    weights = pl.BlockSpec((width, cols), lambda f: (0, f))
    out = pl.BlockSpec((slots, cols), lambda f: (0, f))
    acts = jax.ShapeDtypeStruct((slots, half), BF16)
    return pl.pallas_call(
        expert_kernel,
        grid=(steps,),
        in_specs=[
            whole((slots + TAIL, width)), whole((slots + TAIL, width)),
            weights, weights, weights, weights,
        ]
        + [ANY] * len(ahead),
        out_specs=[
            out, out, out, out,
            whole((slots + TAIL, width)), whole((slots, width)),
            whole((width, slots)), whole((width, slots)),
        ],
        out_shape=[
            acts, acts, acts, acts,
            jax.ShapeDtypeStruct((slots + TAIL, width), BF16),
            jax.ShapeDtypeStruct((slots, width), BF16),
            jax.ShapeDtypeStruct((width, slots), BF16),
            jax.ShapeDtypeStruct((width, slots), BF16),
        ],
        scratch_shapes=[
            pltpu.VMEM((slots, width), BF16),
            pltpu.VMEM((slots, width), F32),
            pltpu.VMEM((slots, width), F32),
        ],
        compiler_params=pltpu.CompilerParams(vmem_limit_bytes=60 * MIB),
        cost_estimate=LIGHT,
        name="expert_chunk",
    )(rows, grads, own_in, own_out, other_in, other_out, *ahead)


def weight_grad_kernel(count, *refs):
    turned = refs[:count]
    acts = refs[count : 2 * count]
    out_ref = refs[-1]
    both_rows = jnp.concatenate([ref[...] for ref in turned], axis=1)
    both_acts = jnp.concatenate([ref[...] for ref in acts], axis=0)
    out_ref[...] = dot_nn(both_rows, both_acts).astype(BF16)


def weight_grad(turned, acts, ahead=()):
    count = len(turned)
    width, slots = turned[0].shape
    half = acts[0].shape[1]
    cols = 512
    return pl.pallas_call(
        functools.partial(weight_grad_kernel, count),
        grid=(half // cols,),
        in_specs=[whole((width, slots))] * count
        + [pl.BlockSpec((slots, cols), lambda f: (0, f))] * count
        + [ANY] * len(ahead),
        out_specs=pl.BlockSpec((width, cols), lambda f: (0, f)),
        out_shape=jax.ShapeDtypeStruct((width, half), BF16),
        compiler_params=pltpu.CompilerParams(vmem_limit_bytes=60 * MIB),
        cost_estimate=LIGHT,
        name="weight_grad",
    )(*turned, *acts, *ahead)


def combine_kernel(count, *refs):
    backs, ends = refs[:count], refs[count : 2 * count]
    (dest_ref, gates_ref, residual_ref, grad_ref, gain_ref, router_ref, w_ref) = refs[
        2 * count : 2 * count + 7
    ]
    (d_residual_ref, branch_ref, mixed_ref, gain_grad, logit_grad, stacked, tails) = refs[-7:]
    slots = backs[0].shape[0]

    @pl.when(pl.program_id(0) == 0)
    def _():
        gain_grad[...] = jnp.zeros_like(gain_grad)
        tails[...] = jnp.zeros_like(tails)
        for index, (back, end) in enumerate(zip(backs, ends)):
            columns = slice(index * slots, (index + 1) * slots)
            stacked[columns, :] = back[...]
            tails[index * TAIL : (index + 1) * TAIL, columns] = end[:, :slots]

    place = lax.broadcasted_iota(jnp.int32, (ROWS, slots), 1)
    lane = lax.broadcasted_iota(jnp.int32, (ROWS, 128), 1)
    dest = as_columns(dest_ref)
    hot = jnp.concatenate(
        [
            (place == dest[:, index : index + 1]).astype(F32).astype(BF16)
            for index in range(count)
        ],
        axis=1,
    )
    d_normed = dot_nn(hot, stacked[...])
    picked = dot_nt(hot, tails[...])
    d_gates = jnp.zeros((ROWS, 128), F32)
    for index in range(count):
        part = picked[:, index * TAIL : index * TAIL + 1]
        for extra in (1, 2):
            part = part + picked[:, index * TAIL + extra : index * TAIL + extra + 1]
        d_gates = jnp.where(lane == index, part, d_gates)
    gates = gates_ref[...]
    inner = jnp.sum(gates * d_gates, axis=1, keepdims=True)
    d_logits = gates * (d_gates - inner)
    logit_grad[...] = d_logits
    for index in range(count):
        d_normed = d_normed + d_logits[:, index : index + 1] * router_ref[index : index + 1, :]
    residual = residual_ref[...]
    scale = lax.rsqrt(jnp.mean(residual * residual, axis=1, keepdims=True) + EPS)
    unit = residual * scale
    scaled = gain_ref[...] * d_normed
    pull = jnp.mean(scaled * unit, axis=1, keepdims=True)
    d_residual = grad_ref[...].astype(F32) + scale * (scaled - unit * pull)
    d_residual_ref[...] = d_residual
    branch = d_residual.astype(BF16)
    branch_ref[...] = branch
    mixed_ref[...] = dot_nt(branch, w_ref[...]).astype(BF16)
    gain_grad[...] += jnp.sum(d_normed * unit, axis=0, keepdims=True)


def combine_back(backs, dest_row, gates, residual, grad, gain, router_rows, w_out, ahead=()):
    rows, width = residual.shape
    count = len(backs)
    slots = backs[0].shape[0] - TAIL
    block = lambda n: pl.BlockSpec((ROWS, n), lambda i: (i, 0))
    return pl.pallas_call(
        functools.partial(combine_kernel, count),
        grid=(rows // ROWS,),
        in_specs=[pl.BlockSpec((slots, width), lambda i: (0, 0))] * count
        + [pl.BlockSpec((TAIL, width), lambda i: (slots // TAIL, 0))] * count
        + [
            pl.BlockSpec((dest_row.shape[0], ROWS), lambda i: (0, i)),
            block(128), block(width), block(width), whole((1, width)),
            whole(router_rows.shape), whole((width, width)),
        ]
        + [ANY] * len(ahead),
        out_specs=[block(width), block(width), block(width), whole((1, width)), block(128)],
        out_shape=[
            jax.ShapeDtypeStruct((rows, width), F32),
            jax.ShapeDtypeStruct((rows, width), BF16),
            jax.ShapeDtypeStruct((rows, width), BF16),
            jax.ShapeDtypeStruct((1, width), F32),
            jax.ShapeDtypeStruct((rows, 128), F32),
        ],
        scratch_shapes=[
            pltpu.VMEM((count * slots, width), BF16),
            pltpu.VMEM((count * TAIL, count * slots), BF16),
        ],
        compiler_params=pltpu.CompilerParams(vmem_limit_bytes=60 * MIB),
        cost_estimate=LIGHT,
        name="combine_back",
    )(*backs, *backs, dest_row, gates, residual, grad, gain, router_rows, w_out, *ahead)


def output_kernel(count, *refs):
    mades = refs[:count]
    dest_ref, gates_ref, residual_ref = refs[count : count + 3]
    out_ref = refs[-1]
    slots = mades[0].shape[0]
    place = lax.broadcasted_iota(jnp.int32, (ROWS, slots), 1)
    dest = as_columns(dest_ref)
    total = residual_ref[...]
    for index, made in enumerate(mades):
        hot = (place == dest[:, index : index + 1]).astype(F32).astype(BF16)
        total = total + gates_ref[:, index : index + 1] * dot_nn(hot, made[...])
    out_ref[...] = total.astype(BF16)


def combine_output(mades, dest_row, gates, residual, ahead=()):
    rows, width = residual.shape
    count = len(mades)
    slots = mades[0].shape[0]
    block = lambda n: pl.BlockSpec((ROWS, n), lambda i: (i, 0))
    return pl.pallas_call(
        functools.partial(output_kernel, count),
        grid=(rows // ROWS,),
        in_specs=[pl.BlockSpec((slots, width), lambda i: (0, 0))] * count
        + [pl.BlockSpec((dest_row.shape[0], ROWS), lambda i: (0, i)), block(128), block(width)]
        + [ANY] * len(ahead),
        out_specs=block(width),
        out_shape=jax.ShapeDtypeStruct((rows, width), BF16),
        compiler_params=pltpu.CompilerParams(vmem_limit_bytes=60 * MIB),
        cost_estimate=LIGHT,
        name="combine_output",
    )(*mades, dest_row, gates, residual, *ahead)


def final_kernel(dqkv_ref, w_ref, tokens_ref, gain_ref, d_residual_ref, *rest):
    out_ref = rest[-1]
    width = tokens_ref.shape[1]
    d_normed = (
        dot_nt(dqkv_ref[0], w_ref[:, :width])
        + dot_nt(dqkv_ref[1], w_ref[:, width : 2 * width])
        + dot_nt(dqkv_ref[2], w_ref[:, 2 * width : 3 * width])
    )
    tokens = tokens_ref[...].astype(F32)
    scale = lax.rsqrt(jnp.mean(tokens * tokens, axis=1, keepdims=True) + EPS)
    unit = tokens * scale
    scaled = gain_ref[...] * d_normed
    pull = jnp.mean(scaled * unit, axis=1, keepdims=True)
    out_ref[...] = d_residual_ref[...] + scale * (scaled - unit * pull)


def final_tokens(d_qkv, w_all, tokens, gain, d_residual, ahead=()):
    rows, width = tokens.shape
    block = lambda n: pl.BlockSpec((ROWS, n), lambda i: (i, 0))
    return pl.pallas_call(
        final_kernel,
        grid=(rows // ROWS,),
        in_specs=[
            pl.BlockSpec((3, ROWS, width), lambda i: (0, i, 0)), whole((width, 3 * width)),
            block(width), whole((1, width)), block(width),
        ]
        + [ANY] * len(ahead),
        out_specs=block(width),
        out_shape=jax.ShapeDtypeStruct((rows, width), F32),
        compiler_params=pltpu.CompilerParams(vmem_limit_bytes=60 * MIB),
        cost_estimate=LIGHT,
        name="final_tokens",
    )(d_qkv, w_all, tokens, gain, d_residual, *ahead)


def qkv_grad_kernel(turned_ref, grad_ref, mixed_ref, branch_ref, extra_ref, *rest):
    keep_ref, send_ref = rest[-2:]
    half, width = keep_ref.shape[0], branch_ref.shape[1]

    def store(made, column):
        keep_ref[:, column : column + made.shape[1]] = made[:half]
        send_ref[:, column : column + made.shape[1]] = made[half:]

    for index in range(4):

        @pl.when(pl.program_id(0) == index)
        def _():
            if index < 3:
                made = dot_nn(turned_ref[...], grad_ref[0])
            else:
                made = dot_nn(mixed_ref[...], branch_ref[...])
                store(extra_ref[...], 4 * width)
            store(made.astype(BF16), index * width)


def qkv_grad(turned, d_qkv, mixed_turned, branch, extra, ahead=()):
    width, rows = turned.shape
    return pl.pallas_call(
        qkv_grad_kernel,
        grid=(4,),
        in_specs=[
            whole((width, rows)),
            pl.BlockSpec((1, rows, width), lambda j: (jnp.minimum(j, 2), 0, 0)),
            whole((width, rows)), whole((rows, width)), whole((width, 128)),
        ]
        + [ANY] * len(ahead),
        out_specs=[whole((width // 2, 4 * width + 128))] * 2,
        out_shape=[jax.ShapeDtypeStruct((width // 2, 4 * width + 128), BF16)] * 2,
        compiler_params=pltpu.CompilerParams(vmem_limit_bytes=60 * MIB),
        cost_estimate=LIGHT,
        name="qkv_grad",
    )(turned, d_qkv, mixed_turned, branch, extra, *ahead)


def pairs_of(size, offset):
    return [(i, i ^ offset) for i in range(size)]


def gather_line(block):
    dp_size = lax.axis_size("dp")
    line = [block]
    for m in range(1, dp_size):
        line.append(lax.ppermute(block, "dp", pairs_of(dp_size, m)))
    return jnp.concatenate(line, axis=0)


def gather_plane(line, ahead):
    fsdp_size = lax.axis_size("fsdp")
    plane = [line]
    for m in range(1, fsdp_size // 2):
        plane.append(lax.ppermute(line, "fsdp", pairs_of(fsdp_size, 2 * m)))
    (plane,) = held([jnp.concatenate(plane, axis=0)], ahead)
    other = lax.ppermute(plane, "fsdp", pairs_of(fsdp_size, 1))
    return plane, other, jnp.concatenate([plane, other], axis=0)


def scatter_pair(keep, send):
    fsdp_size = lax.axis_size("fsdp")
    got = lax.ppermute(send, "fsdp", pairs_of(fsdp_size, 1))
    return (keep.astype(F32) + got.astype(F32)).astype(BF16)


def scatter_plane(plane):
    fsdp_size = lax.axis_size("fsdp")
    rows = 2 * plane.shape[0] // fsdp_size
    line = plane[:rows].astype(F32)
    for m in range(1, fsdp_size // 2):
        got = lax.ppermute(plane[m * rows : (m + 1) * rows], "fsdp", pairs_of(fsdp_size, 2 * m))
        line = line + got.astype(F32)
    return line.astype(BF16)


def scatter_line(line):
    dp_size = lax.axis_size("dp")
    rows = line.shape[0] // dp_size
    total = line[:rows].astype(F32)
    for m in range(1, dp_size):
        got = lax.ppermute(line[m * rows : (m + 1) * rows], "dp", pairs_of(dp_size, m))
        total = total + got.astype(F32)
    return total


def position_matrix(width):
    dp_size, fsdp_size = lax.axis_size("dp"), lax.axis_size("fsdp")
    layer, place = lax.axis_index("dp"), lax.axis_index("fsdp")
    chips = fsdp_size // 2
    rows = width // (dp_size * fsdp_size)
    position = jnp.arange(width, dtype=jnp.int32)
    row = position % rows
    layer_of = (position // rows) % dp_size ^ layer
    chip_of = (position // (rows * dp_size)) % chips ^ (place // 2)
    core_of = position // (rows * dp_size * chips) ^ (place % 2)
    source = ((layer_of * chips + chip_of) * 2 + core_of) * rows + row
    return (position[:, None] == source[None, :]).astype(BF16)


def local(
    tokens_in, w_qkv, w_attn_out, gain_attn, gain_ffn, rel_bias, router, w_in, w_out,
    segment_ids, expert_ids, d_out,
):
    tok_rows, width = tokens_in.shape
    top_count = expert_ids.shape[1]
    fsdp_size = lax.axis_size("fsdp")
    experts = fsdp_size // 2
    slots = min(tok_rows, tok_rows * top_count * 5 // (4 * experts))
    me = lax.axis_index("fsdp") // 2

    own_in = lax.all_gather(w_in, "dp", axis=0, tiled=True)
    own_out = lax.all_gather(w_out, "dp", axis=0, tiled=True)
    small = jnp.concatenate(
        [router, gain_attn[:, None], gain_ffn[:, None], rel_bias[:, None]], axis=1
    )
    small = jnp.pad(small, ((0, 0), (0, 128 - small.shape[1])))
    relative = expert_ids ^ me
    hot = jnp.sum(
        (relative[:, :, None] == jnp.arange(experts, dtype=jnp.int32)).astype(jnp.int32), axis=1
    )
    rank = jnp.cumsum(hot, axis=0) - hot
    dest = jnp.where(hot > 0, rank, -1)
    lines = max(8, experts)
    dest_row = jnp.pad(dest.T, ((0, lines - experts), (0, 0)), constant_values=-1)

    def exchange(pieces):
        return [pieces[0]] + [
            lax.ppermute(pieces[m], "fsdp", pairs_of(fsdp_size, 2 * m)) for m in range(1, experts)
        ]

    line = gather_line(jnp.concatenate([w_qkv, w_attn_out, small], axis=1))
    sent_grads = dispatch(
        experts, dest_row, d_out, jnp.zeros((lines, tok_rows), F32), slots, (line,)
    )
    move = position_matrix(width)
    (tokens_after,) = held([tokens_in], (line,))
    tokens = tokens_after.astype(F32)
    scale = lax.rsqrt(jnp.mean(tokens * tokens, axis=1, keepdims=True) + EPS)
    unit = jnp.dot(tokens_after, move, preferred_element_type=F32) * scale
    plane, plane_rest, full = gather_plane(line, (sent_grads[1], unit))
    grads_in = exchange([sent_grads[0]] + list(held(sent_grads[1:], (plane,))))

    moved_gain = full[:, 4 * width + experts].astype(F32).reshape(1, width)
    columns = jnp.dot(move, full[:, 4 * width :], preferred_element_type=F32).astype(BF16)
    back_qkv = jnp.dot(move, full[:, : 3 * width], preferred_element_type=F32).astype(BF16)
    back_attn = jnp.dot(
        move, full[:, 3 * width : 4 * width], preferred_element_type=F32
    ).astype(BF16)
    by_row = columns.T
    gain_a = by_row[experts : experts + 1].astype(F32)
    gain_f = by_row[experts + 1 : experts + 2].astype(F32)
    table = by_row[experts + 2].reshape(HEADS, BUCKETS)
    bucket_hot = (
        buckets_of(jnp.arange(BLK, dtype=jnp.int32))[:, None]
        == jnp.arange(BUCKETS, dtype=jnp.int32)[None, :]
    )
    near = jnp.dot(table, bucket_hot.T.astype(BF16), preferred_element_type=F32)
    near = near.reshape(HEADS // 2, 2, BLK)
    far = table[:, BUCKETS - 1].astype(F32)
    place = jnp.arange(128, dtype=jnp.int32)
    swap = ((place[:, None] ^ me) == place[None, :]) & (place[:, None] < experts)
    router_cols = jnp.dot(columns, swap.astype(BF16), preferred_element_type=F32).astype(BF16)
    router_rows = router_cols.T[: max(8, experts)].astype(F32)

    normed_attn = (unit * moved_gain).astype(BF16)
    qkv_rows = jnp.dot(normed_attn, full[:, : 3 * width], preferred_element_type=F32).astype(BF16)
    segments = segment_ids.reshape(tok_rows)
    mixed, lse = attention_forward(qkv_rows, segments, near, far, HEADS)
    residual, normed_ffn, gates, gate_row, moved_mixed = post_attention(
        mixed, plane, plane_rest, tokens_in, gain_f, router_cols, dest_row, move,
    )
    sent_rows = dispatch(experts, dest_row, normed_ffn, gate_row, slots, tuple(grads_in[1:]))
    rows_in = exchange(sent_rows)
    (own_in,) = held([own_in], (mixed,))
    (own_out,) = held([own_out], (sent_rows[0],))
    other_in = lax.ppermute(own_in, "fsdp", pairs_of(fsdp_size, 1))
    other_out = lax.ppermute(own_out, "fsdp", pairs_of(fsdp_size, 1))

    chunks, backs = [], []
    for m in range(experts):
        ahead = tuple(backs[1 : m - 1]) + ((chunks[-1][4],) if chunks else ())
        chunks.append(
            expert_chunk(rows_in[m], grads_in[m], own_in, own_out, other_in, other_out, ahead)
        )
        back = chunks[-1][4]
        backs.append(
            lax.ppermute(back, "fsdp", pairs_of(fsdp_size, 2 * m)) if m > 0 else back
        )
    hid_own, hid_other, dpre_own, dpre_other, _, made, rows_turned, gexp_turned = zip(*chunks)

    def owners(pair):
        return lax.psum_scatter(pair, "dp", scatter_dimension=0, tiled=True)

    swapped = pairs_of(fsdp_size, 1)
    normed_turned, mixed_turned = normed_attn.T, moved_mixed.T
    grad_in_own = weight_grad(rows_turned, dpre_own, tuple(backs[-2:-1]))
    grad_out_own = weight_grad(gexp_turned, hid_own, (grad_in_own,))
    grad_in_other = weight_grad(
        rows_turned, dpre_other, (grad_out_own,) + tuple(backs[-1:])
    )
    grad_out_other = weight_grad(gexp_turned, hid_other, (grad_in_other,))
    got_in = lax.ppermute(grad_in_other, "fsdp", swapped)
    (grad_out_other,) = held([grad_out_other], (got_in,))
    got_out = lax.ppermute(grad_out_other, "fsdp", swapped)
    pair_in = (grad_in_own.astype(F32) + got_in.astype(F32)).astype(BF16)
    (got_out,) = held(
        [got_out], (pair_in, back_attn, normed_turned, mixed_turned, router_rows)
    )
    pair_out = (grad_out_own.astype(F32) + got_out.astype(F32)).astype(BF16)
    d_w_in, d_w_out = owners(pair_in), owners(pair_out)
    mades = exchange([made[0]] + list(held(made[1:], (pair_out,))))

    d_residual, d_branch, d_mixed, d_gain_f, d_logits = combine_back(
        backs, dest_row, gates, residual, d_out, gain_f, router_rows, back_attn,
        (pair_out,),
    )
    d_qkv, near_grad, far_grad = attention_backward(
        qkv_rows, d_mixed, mixed, lse, segments, near, far, HEADS
    )
    near_grad, far_grad = held([near_grad, far_grad], tuple(mades[1:]))
    d_router = jnp.dot(normed_ffn.T, d_logits.astype(BF16), preferred_element_type=F32)
    d_router = jnp.dot(d_router, swap.T.astype(F32), precision=lax.Precision.HIGHEST)
    d_table = jnp.dot(
        near_grad.reshape(HEADS, BLK), bucket_hot.astype(F32), precision=lax.Precision.HIGHEST
    )
    last = jnp.arange(BUCKETS, dtype=jnp.int32)[None, :] == BUCKETS - 1
    d_table = d_table + jnp.where(last, far_grad[:, :, :1].reshape(HEADS, 1), 0.0)
    late_cols = jnp.where(place[None, :] == experts, d_gain_f.reshape(width, 1), d_router)
    late_cols = jnp.where(place[None, :] == experts + 1, d_table.reshape(width, 1), late_cols)
    late_cols = jnp.dot(move.T, late_cols.astype(BF16), preferred_element_type=F32)
    late_cols = late_cols.astype(BF16)
    keep, send = qkv_grad(
        normed_turned, d_qkv, mixed_turned, d_branch, late_cols, (d_w_in,)
    )
    keep, send = held([keep, send], (d_w_out,))
    late = scatter_plane(scatter_pair(keep, send))
    block_out = combine_output(mades, dest_row, gates, residual)
    d_tokens = final_tokens(d_qkv, back_qkv, tokens_in, gain_a, d_residual, (block_out,))
    (late,) = held([late], (d_tokens,))
    late = scatter_line(late)
    own_qkv = late[:, : 3 * width]
    own_gain_a = jnp.sum(own_qkv * w_qkv.astype(F32), axis=1) / gain_attn.astype(F32)
    return (
        block_out,
        d_tokens,
        own_qkv,
        late[:, 3 * width : 4 * width],
        own_gain_a,
        late[:, 4 * width + experts],
        late[:, 4 * width + experts + 1],
        late[:, 4 * width : 4 * width + experts],
        d_w_in.astype(F32),
        d_w_out.astype(F32),
    )


def solution(mesh):
    both = P(("dp", "fsdp"), None)
    line = P(("dp", "fsdp"))
    tiles = P("dp", "fsdp")
    return jax.shard_map(
        local,
        mesh=mesh,
        in_specs=(both, both, both, line, line, line, both, tiles, tiles, both, both, both),
        out_specs=(both, both, both, both, line, line, line, both, tiles, tiles),
        check_vma=False,
    )
```

```python
import functools
import math

import jax
import jax.numpy as jnp
from jax import lax
from jax.experimental import pallas as pl
from jax.experimental.pallas import tpu as pltpu
from jax.sharding import PartitionSpec as P

NEG = -1e30
BLK = 256
SPAN = 2
F32 = jnp.float32
BF16 = jnp.bfloat16
LIGHT = pl.CostEstimate(flops=1000, bytes_accessed=1000, transcendentals=0)


def dot_nt(a, b):
    return lax.dot_general(a, b, (((1,), (1,)), ((), ())), preferred_element_type=F32)


def dot_nn(a, b):
    return lax.dot_general(a, b, (((1,), (0,)), ((), ())), preferred_element_type=F32)


def fill_masks(mask, seg_row, seg_col, blocks):
    key_place = lax.broadcasted_iota(jnp.int32, (BLK, BLK), 0)
    row_place = lax.broadcasted_iota(jnp.int32, (BLK, BLK), 1)
    for kb in range(blocks):
        keys = seg_col[kb * BLK : (kb + 1) * BLK, :]
        for step in range(min(SPAN + 1, blocks - kb)):
            rows = seg_row[:, (kb + step) * BLK : (kb + step + 1) * BLK]
            seen = keys == rows
            if step == 0:
                seen = seen & (row_place >= key_place)
            mask[kb, step] = jnp.where(seen, 0.0, NEG)


def bias_tiles(near_row, far_value):
    key_place = lax.broadcasted_iota(jnp.int32, (BLK, BLK), 0)
    row_place = lax.broadcasted_iota(jnp.int32, (BLK, BLK), 1)
    rolled = pltpu.roll(
        jnp.broadcast_to(near_row, (BLK, BLK)), 0, 1, stride=1, stride_axis=0
    )
    return rolled, jnp.where(row_place < key_place, rolled, far_value)


def head_lanes(values, half):
    lane = lax.broadcasted_iota(jnp.int32, values.shape, 1)
    keep = (lane >= 64) if half else (lane < 64)
    return jnp.where(keep, values, jnp.zeros_like(values))


def attn_fwd_kernel(
    far_ref, q_ref, k_ref, v_ref, near_ref, seg_row, seg_col, *rest
):
    o_ref, lse_ref, mask, turned = rest[-4:]
    pair = pl.program_id(0)
    length = q_ref.shape[0]
    blocks = length // BLK

    @pl.when(pair == 0)
    def _():
        fill_masks(mask, seg_row, seg_col, blocks)

    v_turned = v_ref[...].T
    ones = jnp.ones((16, length), BF16)
    for half in range(2):
        far_value = far_ref[pair * 2 + half]
        diag, below = bias_tiles(near_ref[0, half : half + 1, :], far_value)
        keys = head_lanes(k_ref[...], half)
        values = jnp.concatenate([v_turned[64 * half : 64 * half + 64], ones], axis=0)
        for a in range(blocks):
            first = max(0, a - SPAN)
            q_rows = q_ref[a * BLK : (a + 1) * BLK, :] * jnp.asarray(0.125, BF16)
            parts = []
            for kb in range(first, a + 1):
                part = dot_nt(keys[kb * BLK : (kb + 1) * BLK], q_rows)
                bias = (diag, below, far_value)[a - kb]
                parts.append(part + bias + mask[kb, a - kb])
            peak = functools.reduce(
                jnp.maximum, [jnp.max(part, axis=0, keepdims=True) for part in parts]
            )
            weights = jnp.concatenate(
                [jnp.exp(part - peak).astype(BF16) for part in parts], axis=0
            )
            made = dot_nn(values[:, first * BLK : (a + 1) * BLK], weights)
            total = made[64:65]
            turned[64 * half : 64 * half + 64, a * BLK : (a + 1) * BLK] = made[:64] / total
            lse_ref[0, half : half + 1, a * BLK : (a + 1) * BLK] = peak + jnp.log(total)
    o_ref[...] = turned[...].T.astype(BF16)


def attn_bwd_kernel(
    far_ref, q_ref, k_ref, v_ref, g_ref, o_ref, lse_ref, near_ref, seg_row, seg_col, *rest
):
    d_ref, near_grad, far_grad, mask, turned = rest[-5:]
    pair = pl.program_id(0)
    length = q_ref.shape[0]
    blocks = length // BLK

    @pl.when(pair == 0)
    def _():
        fill_masks(mask, seg_row, seg_col, blocks)

    scaled = q_ref[...] * jnp.asarray(0.125, BF16)
    k_turned = k_ref[...].T
    ones = jnp.ones((16, length), BF16)
    inner = (g_ref[...].astype(F32) * o_ref[...].astype(F32)).T
    key_place = lax.broadcasted_iota(jnp.int32, (BLK, BLK), 0)
    row_place = lax.broadcasted_iota(jnp.int32, (BLK, BLK), 1)
    key_grads = [None] * blocks
    value_grads = [None] * blocks
    for half in range(2):
        far_value = far_ref[pair * 2 + half]
        diag, below = bias_tiles(near_ref[0, half : half + 1, :], far_value)
        keys = head_lanes(k_ref[...], half)
        values = head_lanes(v_ref[...], half)
        q_own = head_lanes(scaled, half)
        g_own = head_lanes(g_ref[...], half)
        keys_turned = jnp.concatenate([k_turned[64 * half : 64 * half + 64], ones], axis=0)
        delta = jnp.sum(inner[64 * half : 64 * half + 64], axis=0, keepdims=True)
        lse = lse_ref[0, half : half + 1, :]
        diag_grad = jnp.zeros((BLK, BLK), F32)
        below_grad = jnp.zeros((BLK, BLK), F32)
        turned[...] = jnp.zeros_like(turned)
        for kb in range(blocks):
            last = min(kb + SPAN + 1, blocks)
            k_rows = keys[kb * BLK : (kb + 1) * BLK]
            v_rows = values[kb * BLK : (kb + 1) * BLK]
            probs, grads = [], []
            for a in range(kb, last):
                rows = slice(a * BLK, (a + 1) * BLK)
                score = dot_nt(k_rows, scaled[rows])
                d_prob = dot_nt(v_rows, g_ref[rows, :])
                bias = (diag, below, far_value)[a - kb]
                prob = jnp.exp(score + bias + mask[kb, a - kb] - lse[:, rows])
                d_score = prob * (d_prob - delta[:, rows])
                if a == kb:
                    diag_grad = diag_grad + d_score
                elif a == kb + 1:
                    below_grad = below_grad + d_score
                probs.append(prob.astype(BF16))
                grads.append(d_score.astype(BF16))
            wide = slice(kb * BLK, last * BLK)
            prob_wide = jnp.concatenate(probs, axis=1)
            grad_wide = jnp.concatenate(grads, axis=1)
            value_grad = dot_nn(prob_wide, g_own[wide])
            key_grad = dot_nn(grad_wide, q_own[wide])
            turned[:, wide] += dot_nn(keys_turned[:, kb * BLK : (kb + 1) * BLK], grad_wide)
            if half == 0:
                value_grads[kb], key_grads[kb] = value_grad, key_grad
            else:
                rows = slice(kb * BLK, (kb + 1) * BLK)
                d_ref[2, rows, :] = (value_grads[kb] + value_grad).astype(BF16)
                d_ref[1, rows, :] = (key_grads[kb] + key_grad).astype(BF16)
        part = (turned[:64] * 0.125).T
        if half == 0:
            first_part = part
        else:
            d_ref[0] = jnp.concatenate([first_part, part], axis=1).astype(BF16)
        by_offset = diag_grad + jnp.where(row_place < key_place, below_grad, 0.0)
        for bit in range(8):
            by_offset = jnp.where(
                ((key_place >> bit) & 1) == 1,
                pltpu.roll(by_offset, BLK - (1 << bit), 1),
                by_offset,
            )
        near = jnp.sum(by_offset, axis=0, keepdims=True)
        near_grad[0, half : half + 1, :] = near
        everything = jnp.sum(turned[64:65, :], axis=1, keepdims=True)
        rest = everything - jnp.sum(near, axis=1, keepdims=True)
        far_grad[0, half : half + 1, :] = jnp.broadcast_to(rest, (1, 128))


def attention_specs(length, pairs):
    def column(offset):
        return pl.BlockSpec((length, 128), lambda p, far: (0, p + offset))

    return column


def attention_forward(qkv_rows, segments, near, far, heads, ahead=()):
    length = qkv_rows.shape[0]
    pairs = heads // 2
    width = heads * 64
    column = attention_specs(length, pairs)
    blocks = length // BLK
    return pl.pallas_call(
        attn_fwd_kernel,
        grid_spec=pltpu.PrefetchScalarGridSpec(
            num_scalar_prefetch=1,
            grid=(pairs,),
            in_specs=[
                column(0),
                column(pairs),
                column(2 * pairs),
                pl.BlockSpec((1, 2, BLK), lambda p, far: (p, 0, 0)),
                pl.BlockSpec((1, length), lambda p, far: (0, 0)),
                pl.BlockSpec((length, 1), lambda p, far: (0, 0)),
            ]
            + [pl.BlockSpec(memory_space=pl.ANY)] * len(ahead),
            out_specs=[
                column(0),
                pl.BlockSpec((1, 2, length), lambda p, far: (p, 0, 0)),
            ],
            scratch_shapes=[
                pltpu.VMEM((blocks, SPAN + 1, BLK, BLK), F32),
                pltpu.VMEM((128, length), F32),
            ],
        ),
        out_shape=[
            jax.ShapeDtypeStruct((length, width), BF16),
            jax.ShapeDtypeStruct((pairs, 2, length), F32),
        ],
        compiler_params=pltpu.CompilerParams(vmem_limit_bytes=60 * 1024 * 1024),
        cost_estimate=LIGHT,
        name="attention_forward",
    )(far, qkv_rows, qkv_rows, qkv_rows, near, segments.reshape(1, length), segments.reshape(length, 1), *ahead)


def attention_backward(qkv_rows, d_mixed, mixed, lse, segments, near, far, heads, ahead=()):
    length = qkv_rows.shape[0]
    pairs = heads // 2
    width = heads * 64
    column = attention_specs(length, pairs)
    blocks = length // BLK
    small = lambda n: pl.BlockSpec((1, 2, n), lambda p, far: (p, 0, 0))
    return pl.pallas_call(
        attn_bwd_kernel,
        grid_spec=pltpu.PrefetchScalarGridSpec(
            num_scalar_prefetch=1,
            grid=(pairs,),
            in_specs=[
                column(0),
                column(pairs),
                column(2 * pairs),
                column(0),
                column(0),
                small(length),
                small(BLK),
                pl.BlockSpec((1, length), lambda p, far: (0, 0)),
                pl.BlockSpec((length, 1), lambda p, far: (0, 0)),
            ]
            + [pl.BlockSpec(memory_space=pl.ANY)] * len(ahead),
            out_specs=[
                pl.BlockSpec((3, length, 128), lambda p, far: (0, 0, p)),
                small(BLK),
                small(128),
            ],
            scratch_shapes=[
                pltpu.VMEM((blocks, SPAN + 1, BLK, BLK), F32),
                pltpu.VMEM((80, length), F32),
            ],
        ),
        out_shape=[
            jax.ShapeDtypeStruct((3, length, width), BF16),
            jax.ShapeDtypeStruct((pairs, 2, BLK), F32),
            jax.ShapeDtypeStruct((pairs, 2, 128), F32),
        ],
        compiler_params=pltpu.CompilerParams(vmem_limit_bytes=60 * 1024 * 1024),
        cost_estimate=LIGHT,
        name="attention_backward",
    )(
        far, qkv_rows, qkv_rows, qkv_rows, d_mixed, mixed, lse, near,
        segments.reshape(1, length), segments.reshape(length, 1), *ahead,
    )


HEADS = 12
BUCKETS = 64
MAX_DIST = 128
EPS = 1e-06
ROWS = 256
TAIL = 16
COEF = math.sqrt(2.0 / math.pi)
CUBIC = 0.044715
MIB = 1024 * 1024


def bucket_bounds(bucket_count, max_distance):
    halfway = bucket_count // 2
    bounds = []
    for bucket in range(bucket_count):
        if bucket < halfway:
            bounds.append(bucket)
        else:
            bounds.append(
                int(math.ceil(halfway * (max_distance / halfway) ** ((bucket - halfway) / halfway)))
            )
    return bounds


def buckets_of(distance):
    limits = jnp.array(bucket_bounds(BUCKETS, MAX_DIST), dtype=jnp.int32)
    reached = (distance[:, None] >= limits[None, :]).astype(jnp.int32)
    return jnp.sum(reached, axis=1) - 1


def whole(shape):
    return pl.BlockSpec(shape, lambda *_: (0,) * len(shape))


def split_three(values):
    high = values.astype(BF16)
    rest = values - high.astype(F32)
    middle = rest.astype(BF16)
    low = (rest - middle.astype(F32)).astype(BF16)
    return high, middle, low


ANY = pl.BlockSpec(memory_space=pl.ANY)


def dispatch_kernel(experts, dest_ref, values_ref, gate_ref, *rest):
    out_refs = rest[-experts:]
    slots = out_refs[0].shape[0] - TAIL
    tokens = values_ref.shape[0]
    own = pl.ds(pl.program_id(0), 1)
    place = lax.broadcasted_iota(jnp.int32, (slots, tokens), 0)
    hot = (place == dest_ref[own, :]).astype(F32).astype(BF16)
    rows = dot_nn(hot, values_ref[...]).astype(BF16)
    pieces = split_three(jnp.broadcast_to(gate_ref[own, :], (TAIL, tokens)))
    line = lax.broadcasted_iota(jnp.int32, (TAIL, tokens), 0)
    stacked = jnp.zeros((TAIL, tokens), F32)
    for index, piece in enumerate(pieces):
        stacked = jnp.where(line == index, piece.astype(F32), stacked)
    tail = dot_nt(stacked.astype(BF16), hot).astype(BF16)
    for index, out_ref in enumerate(out_refs):

        @pl.when(pl.program_id(0) == index)
        def _():
            out_ref[:slots, :] = rows
            out_ref[slots:, :] = jnp.zeros((TAIL, out_ref.shape[1]), BF16)
            out_ref[slots:, :slots] = tail


def dispatch(experts, dest_row, values, gate_row, slots, ahead=()):
    tokens, width = values.shape
    return pl.pallas_call(
        functools.partial(dispatch_kernel, experts),
        grid=(experts,),
        in_specs=[
            whole(dest_row.shape), whole((tokens, width)), whole(gate_row.shape),
        ]
        + [ANY] * len(ahead),
        out_specs=[whole((slots + TAIL, width))] * experts,
        out_shape=[jax.ShapeDtypeStruct((slots + TAIL, width), BF16)] * experts,
        compiler_params=pltpu.CompilerParams(vmem_limit_bytes=60 * MIB),
        cost_estimate=LIGHT,
        name="dispatch_rows",
    )(dest_row, values, gate_row, *ahead)


def nothing_kernel(*refs):
    pass


def held(values, ahead):
    count = len(values)
    return pl.pallas_call(
        nothing_kernel,
        in_specs=[ANY] * (count + len(ahead)),
        out_specs=[ANY] * count,
        out_shape=[jax.ShapeDtypeStruct(value.shape, value.dtype) for value in values],
        input_output_aliases={index: index for index in range(count)},
        cost_estimate=LIGHT,
        name="held",
    )(*values, *ahead)


def as_columns(ref):
    rows = ref[...].astype(F32)
    filler = jnp.full((128 - rows.shape[0], rows.shape[1]), -1.0, F32)
    return jnp.concatenate([rows, filler], axis=0).T.astype(jnp.int32)


def post_kernel(
    mixed_ref, w_ref, w_rest, tokens_ref, gain_ref, router_ref, dest_ref, move_ref, *rest
):
    residual_ref, normed_ref, gates_ref, turned_ref, moved_ref = rest[-5:]
    half = w_ref.shape[0]
    moved = dot_nn(mixed_ref[...], move_ref[...]).astype(BF16)
    moved_ref[...] = moved
    residual = dot_nn(moved[:, :half], w_ref[...]) + dot_nn(moved[:, half:], w_rest[...])
    residual = tokens_ref[...].astype(F32) + residual
    residual_ref[...] = residual
    scale = lax.rsqrt(jnp.mean(residual * residual, axis=1, keepdims=True) + EPS)
    normed = (residual * scale * gain_ref[...]).astype(BF16)
    normed_ref[...] = normed
    logits = dot_nn(normed, router_ref[...])
    chosen = as_columns(dest_ref) >= 0
    logits = jnp.where(chosen, logits, NEG)
    peak = jnp.max(logits, axis=1, keepdims=True)
    weights = jnp.where(chosen, jnp.exp(logits - peak), 0.0)
    gates = weights / jnp.sum(weights, axis=1, keepdims=True)
    gates_ref[...] = gates
    turned_ref[...] = gates.T[: turned_ref.shape[0]]


def post_attention(mixed, w_top, w_rest, tokens, gain, router, dest_row, move, ahead=()):
    rows, width = tokens.shape
    lines = dest_row.shape[0]
    block = lambda n: pl.BlockSpec((ROWS, n), lambda i: (i, 0))
    return pl.pallas_call(
        post_kernel,
        grid=(rows // ROWS,),
        in_specs=[
            block(width), pl.BlockSpec((width // 2, width), lambda i: (0, 3)),
            pl.BlockSpec((width // 2, width), lambda i: (0, 3)), block(width),
            whole((1, width)), whole((width, 128)),
            pl.BlockSpec((lines, ROWS), lambda i: (0, i)), whole((width, width)),
        ]
        + [ANY] * len(ahead),
        out_specs=[
            block(width), block(width), block(128),
            pl.BlockSpec((lines, ROWS), lambda i: (0, i)), block(width),
        ],
        out_shape=[
            jax.ShapeDtypeStruct((rows, width), F32),
            jax.ShapeDtypeStruct((rows, width), BF16),
            jax.ShapeDtypeStruct((rows, 128), F32),
            jax.ShapeDtypeStruct((lines, rows), F32),
            jax.ShapeDtypeStruct((rows, width), BF16),
        ],
        compiler_params=pltpu.CompilerParams(vmem_limit_bytes=60 * MIB),
        cost_estimate=LIGHT,
        name="post_attention",
    )(mixed, w_top, w_rest, tokens, gain, router, dest_row, move, *ahead)


def expert_kernel(
    rows_ref, grads_ref, in_own, out_own, in_other, out_other, *rest
):
    hid_own, hid_other, dpre_own, dpre_other, back_ref, made_ref = rest[-11:-5]
    rows_turned, gexp_turned, gexp, made_sum, back_sum = rest[-5:]
    step = pl.program_id(0)
    slots = gexp.shape[0]

    @pl.when(step == 0)
    def _():
        turned = rows_ref[slots:, :slots].astype(F32).T
        gate = jnp.sum(turned, axis=1, keepdims=True)
        gexp[...] = (grads_ref[:slots, :].astype(F32) * gate).astype(BF16)
        gexp_turned[...] = gexp[...].T
        rows_turned[...] = rows_ref[:slots, :].T
        made_sum[...] = jnp.zeros_like(made_sum)
        back_sum[...] = jnp.zeros_like(back_sum)

    rows = rows_ref[:slots, :]
    hiddens, d_pres = [], []
    for w_in, w_out, hid, dpre in (
        (in_own, out_own, hid_own, dpre_own),
        (in_other, out_other, hid_other, dpre_other),
    ):
        pre = dot_nn(rows, w_in[...])
        d_hidden = dot_nn(gexp[...], w_out[...])
        square = pre * pre
        half = 0.5 + 0.5 * jnp.tanh(pre * (COEF + COEF * CUBIC * square))
        hidden = pre * half
        slope = half + hidden * (1.0 - half) * (2.0 * COEF + 6.0 * COEF * CUBIC * square)
        hidden_low = hidden.astype(BF16)
        d_pre = (d_hidden * slope).astype(BF16)
        hid[...] = hidden_low
        dpre[...] = d_pre
        hiddens.append(hidden_low)
        d_pres.append(d_pre)
    both_out = jnp.concatenate([out_own[...], out_other[...]], axis=1)
    both_in = jnp.concatenate([in_own[...], in_other[...]], axis=1)
    made_sum[...] += dot_nt(jnp.concatenate(hiddens, axis=1), both_out)
    back_sum[...] += dot_nt(jnp.concatenate(d_pres, axis=1), both_in)

    @pl.when(step == pl.num_programs(0) - 1)
    def _():
        made = made_sum[...]
        made_ref[...] = made.astype(BF16)
        back_ref[:slots, :] = back_sum[...].astype(BF16)
        by_gate = jnp.sum(grads_ref[:slots, :].astype(F32) * made, axis=1, keepdims=True)
        pieces = split_three(jnp.broadcast_to(by_gate, (slots, 128)))
        lane = lax.broadcasted_iota(jnp.int32, (slots, 128), 1)
        stacked = jnp.zeros((slots, 128), F32)
        for index, piece in enumerate(pieces):
            stacked = jnp.where(lane == index, piece.astype(F32), stacked)
        back_ref[slots:, :] = jnp.zeros((TAIL, back_ref.shape[1]), BF16)
        back_ref[slots:, :slots] = stacked.T[:TAIL].astype(BF16)


def expert_chunk(rows, grads, own_in, own_out, other_in, other_out, ahead=()):
    slots, width = rows.shape[0] - TAIL, rows.shape[1]
    half = own_in.shape[1]
    cols = 256
    steps = half // cols
    weights = pl.BlockSpec((width, cols), lambda f: (0, f))
    out = pl.BlockSpec((slots, cols), lambda f: (0, f))
    acts = jax.ShapeDtypeStruct((slots, half), BF16)
    return pl.pallas_call(
        expert_kernel,
        grid=(steps,),
        in_specs=[
            whole((slots + TAIL, width)), whole((slots + TAIL, width)),
            weights, weights, weights, weights,
        ]
        + [ANY] * len(ahead),
        out_specs=[
            out, out, out, out,
            whole((slots + TAIL, width)), whole((slots, width)),
            whole((width, slots)), whole((width, slots)),
        ],
        out_shape=[
            acts, acts, acts, acts,
            jax.ShapeDtypeStruct((slots + TAIL, width), BF16),
            jax.ShapeDtypeStruct((slots, width), BF16),
            jax.ShapeDtypeStruct((width, slots), BF16),
            jax.ShapeDtypeStruct((width, slots), BF16),
        ],
        scratch_shapes=[
            pltpu.VMEM((slots, width), BF16),
            pltpu.VMEM((slots, width), F32),
            pltpu.VMEM((slots, width), F32),
        ],
        compiler_params=pltpu.CompilerParams(vmem_limit_bytes=60 * MIB),
        cost_estimate=LIGHT,
        name="expert_chunk",
    )(rows, grads, own_in, own_out, other_in, other_out, *ahead)


def weight_grad_kernel(count, *refs):
    turned = refs[:count]
    acts = refs[count : 2 * count]
    out_ref = refs[-1]
    both_rows = jnp.concatenate([ref[...] for ref in turned], axis=1)
    both_acts = jnp.concatenate([ref[...] for ref in acts], axis=0)
    out_ref[...] = dot_nn(both_rows, both_acts).astype(BF16)


def weight_grad(turned, acts, ahead=()):
    count = len(turned)
    width, slots = turned[0].shape
    half = acts[0].shape[1]
    cols = 512
    return pl.pallas_call(
        functools.partial(weight_grad_kernel, count),
        grid=(half // cols,),
        in_specs=[whole((width, slots))] * count
        + [pl.BlockSpec((slots, cols), lambda f: (0, f))] * count
        + [ANY] * len(ahead),
        out_specs=pl.BlockSpec((width, cols), lambda f: (0, f)),
        out_shape=jax.ShapeDtypeStruct((width, half), BF16),
        compiler_params=pltpu.CompilerParams(vmem_limit_bytes=60 * MIB),
        cost_estimate=LIGHT,
        name="weight_grad",
    )(*turned, *acts, *ahead)


def combine_kernel(count, *refs):
    backs, ends = refs[:count], refs[count : 2 * count]
    (dest_ref, gates_ref, residual_ref, grad_ref, gain_ref, router_ref, w_ref) = refs[
        2 * count : 2 * count + 7
    ]
    (d_residual_ref, branch_ref, mixed_ref, gain_grad, logit_grad, stacked, tails) = refs[-7:]
    slots = backs[0].shape[0]

    @pl.when(pl.program_id(0) == 0)
    def _():
        gain_grad[...] = jnp.zeros_like(gain_grad)
        tails[...] = jnp.zeros_like(tails)
        for index, (back, end) in enumerate(zip(backs, ends)):
            columns = slice(index * slots, (index + 1) * slots)
            stacked[columns, :] = back[...]
            tails[index * TAIL : (index + 1) * TAIL, columns] = end[:, :slots]

    place = lax.broadcasted_iota(jnp.int32, (ROWS, slots), 1)
    lane = lax.broadcasted_iota(jnp.int32, (ROWS, 128), 1)
    dest = as_columns(dest_ref)
    hot = jnp.concatenate(
        [
            (place == dest[:, index : index + 1]).astype(F32).astype(BF16)
            for index in range(count)
        ],
        axis=1,
    )
    d_normed = dot_nn(hot, stacked[...])
    picked = dot_nt(hot, tails[...])
    d_gates = jnp.zeros((ROWS, 128), F32)
    for index in range(count):
        part = picked[:, index * TAIL : index * TAIL + 1]
        for extra in (1, 2):
            part = part + picked[:, index * TAIL + extra : index * TAIL + extra + 1]
        d_gates = jnp.where(lane == index, part, d_gates)
    gates = gates_ref[...]
    inner = jnp.sum(gates * d_gates, axis=1, keepdims=True)
    d_logits = gates * (d_gates - inner)
    logit_grad[...] = d_logits
    for index in range(count):
        d_normed = d_normed + d_logits[:, index : index + 1] * router_ref[index : index + 1, :]
    residual = residual_ref[...]
    scale = lax.rsqrt(jnp.mean(residual * residual, axis=1, keepdims=True) + EPS)
    unit = residual * scale
    scaled = gain_ref[...] * d_normed
    pull = jnp.mean(scaled * unit, axis=1, keepdims=True)
    d_residual = grad_ref[...].astype(F32) + scale * (scaled - unit * pull)
    d_residual_ref[...] = d_residual
    branch = d_residual.astype(BF16)
    branch_ref[...] = branch
    mixed_ref[...] = dot_nt(branch, w_ref[...]).astype(BF16)
    gain_grad[...] += jnp.sum(d_normed * unit, axis=0, keepdims=True)


def combine_back(backs, dest_row, gates, residual, grad, gain, router_rows, w_out, ahead=()):
    rows, width = residual.shape
    count = len(backs)
    slots = backs[0].shape[0] - TAIL
    block = lambda n: pl.BlockSpec((ROWS, n), lambda i: (i, 0))
    return pl.pallas_call(
        functools.partial(combine_kernel, count),
        grid=(rows // ROWS,),
        in_specs=[pl.BlockSpec((slots, width), lambda i: (0, 0))] * count
        + [pl.BlockSpec((TAIL, width), lambda i: (slots // TAIL, 0))] * count
        + [
            pl.BlockSpec((dest_row.shape[0], ROWS), lambda i: (0, i)),
            block(128), block(width), block(width), whole((1, width)),
            whole(router_rows.shape), whole((width, width)),
        ]
        + [ANY] * len(ahead),
        out_specs=[block(width), block(width), block(width), whole((1, width)), block(128)],
        out_shape=[
            jax.ShapeDtypeStruct((rows, width), F32),
            jax.ShapeDtypeStruct((rows, width), BF16),
            jax.ShapeDtypeStruct((rows, width), BF16),
            jax.ShapeDtypeStruct((1, width), F32),
            jax.ShapeDtypeStruct((rows, 128), F32),
        ],
        scratch_shapes=[
            pltpu.VMEM((count * slots, width), BF16),
            pltpu.VMEM((count * TAIL, count * slots), BF16),
        ],
        compiler_params=pltpu.CompilerParams(vmem_limit_bytes=60 * MIB),
        cost_estimate=LIGHT,
        name="combine_back",
    )(*backs, *backs, dest_row, gates, residual, grad, gain, router_rows, w_out, *ahead)


def output_kernel(count, *refs):
    mades = refs[:count]
    dest_ref, gates_ref, residual_ref = refs[count : count + 3]
    out_ref = refs[-1]
    slots = mades[0].shape[0]
    place = lax.broadcasted_iota(jnp.int32, (ROWS, slots), 1)
    dest = as_columns(dest_ref)
    total = residual_ref[...]
    for index, made in enumerate(mades):
        hot = (place == dest[:, index : index + 1]).astype(F32).astype(BF16)
        total = total + gates_ref[:, index : index + 1] * dot_nn(hot, made[...])
    out_ref[...] = total.astype(BF16)


def combine_output(mades, dest_row, gates, residual, ahead=()):
    rows, width = residual.shape
    count = len(mades)
    slots = mades[0].shape[0]
    block = lambda n: pl.BlockSpec((ROWS, n), lambda i: (i, 0))
    return pl.pallas_call(
        functools.partial(output_kernel, count),
        grid=(rows // ROWS,),
        in_specs=[pl.BlockSpec((slots, width), lambda i: (0, 0))] * count
        + [pl.BlockSpec((dest_row.shape[0], ROWS), lambda i: (0, i)), block(128), block(width)]
        + [ANY] * len(ahead),
        out_specs=block(width),
        out_shape=jax.ShapeDtypeStruct((rows, width), BF16),
        compiler_params=pltpu.CompilerParams(vmem_limit_bytes=60 * MIB),
        cost_estimate=LIGHT,
        name="combine_output",
    )(*mades, dest_row, gates, residual, *ahead)


def final_kernel(dqkv_ref, w_ref, tokens_ref, gain_ref, d_residual_ref, *rest):
    out_ref = rest[-1]
    width = tokens_ref.shape[1]
    d_normed = (
        dot_nt(dqkv_ref[0], w_ref[:, :width])
        + dot_nt(dqkv_ref[1], w_ref[:, width : 2 * width])
        + dot_nt(dqkv_ref[2], w_ref[:, 2 * width : 3 * width])
    )
    tokens = tokens_ref[...].astype(F32)
    scale = lax.rsqrt(jnp.mean(tokens * tokens, axis=1, keepdims=True) + EPS)
    unit = tokens * scale
    scaled = gain_ref[...] * d_normed
    pull = jnp.mean(scaled * unit, axis=1, keepdims=True)
    out_ref[...] = d_residual_ref[...] + scale * (scaled - unit * pull)


def final_tokens(d_qkv, w_all, tokens, gain, d_residual, ahead=()):
    rows, width = tokens.shape
    block = lambda n: pl.BlockSpec((ROWS, n), lambda i: (i, 0))
    return pl.pallas_call(
        final_kernel,
        grid=(rows // ROWS,),
        in_specs=[
            pl.BlockSpec((3, ROWS, width), lambda i: (0, i, 0)), whole((width, 3 * width)),
            block(width), whole((1, width)), block(width),
        ]
        + [ANY] * len(ahead),
        out_specs=block(width),
        out_shape=jax.ShapeDtypeStruct((rows, width), F32),
        compiler_params=pltpu.CompilerParams(vmem_limit_bytes=60 * MIB),
        cost_estimate=LIGHT,
        name="final_tokens",
    )(d_qkv, w_all, tokens, gain, d_residual, *ahead)


def qkv_grad_kernel(turned_ref, grad_ref, mixed_ref, branch_ref, extra_ref, *rest):
    keep_ref, send_ref = rest[-2:]
    half, width = keep_ref.shape[0], branch_ref.shape[1]

    def store(made, column):
        keep_ref[:, column : column + made.shape[1]] = made[:half]
        send_ref[:, column : column + made.shape[1]] = made[half:]

    for index in range(4):

        @pl.when(pl.program_id(0) == index)
        def _():
            if index < 3:
                made = dot_nn(turned_ref[...], grad_ref[0])
            else:
                made = dot_nn(mixed_ref[...], branch_ref[...])
                store(extra_ref[...], 4 * width)
            store(made.astype(BF16), index * width)


def qkv_grad(turned, d_qkv, mixed_turned, branch, extra, ahead=()):
    width, rows = turned.shape
    return pl.pallas_call(
        qkv_grad_kernel,
        grid=(4,),
        in_specs=[
            whole((width, rows)),
            pl.BlockSpec((1, rows, width), lambda j: (jnp.minimum(j, 2), 0, 0)),
            whole((width, rows)), whole((rows, width)), whole((width, 128)),
        ]
        + [ANY] * len(ahead),
        out_specs=[whole((width // 2, 4 * width + 128))] * 2,
        out_shape=[jax.ShapeDtypeStruct((width // 2, 4 * width + 128), BF16)] * 2,
        compiler_params=pltpu.CompilerParams(vmem_limit_bytes=60 * MIB),
        cost_estimate=LIGHT,
        name="qkv_grad",
    )(turned, d_qkv, mixed_turned, branch, extra, *ahead)


def pairs_of(size, offset):
    return [(i, i ^ offset) for i in range(size)]


def gather_line(block):
    dp_size = lax.axis_size("dp")
    line = [block]
    for m in range(1, dp_size):
        line.append(lax.ppermute(block, "dp", pairs_of(dp_size, m)))
    return jnp.concatenate(line, axis=0)


def gather_plane(line, ahead):
    fsdp_size = lax.axis_size("fsdp")
    plane = [line]
    for m in range(1, fsdp_size // 2):
        plane.append(lax.ppermute(line, "fsdp", pairs_of(fsdp_size, 2 * m)))
    (plane,) = held([jnp.concatenate(plane, axis=0)], ahead)
    other = lax.ppermute(plane, "fsdp", pairs_of(fsdp_size, 1))
    return plane, other, jnp.concatenate([plane, other], axis=0)


def scatter_pair(keep, send):
    fsdp_size = lax.axis_size("fsdp")
    got = lax.ppermute(send, "fsdp", pairs_of(fsdp_size, 1))
    return (keep.astype(F32) + got.astype(F32)).astype(BF16)


def scatter_plane(plane):
    fsdp_size = lax.axis_size("fsdp")
    rows = 2 * plane.shape[0] // fsdp_size
    line = plane[:rows].astype(F32)
    for m in range(1, fsdp_size // 2):
        got = lax.ppermute(plane[m * rows : (m + 1) * rows], "fsdp", pairs_of(fsdp_size, 2 * m))
        line = line + got.astype(F32)
    return line.astype(BF16)


def scatter_line(line):
    dp_size = lax.axis_size("dp")
    rows = line.shape[0] // dp_size
    total = line[:rows].astype(F32)
    for m in range(1, dp_size):
        got = lax.ppermute(line[m * rows : (m + 1) * rows], "dp", pairs_of(dp_size, m))
        total = total + got.astype(F32)
    return total


def position_matrix(width):
    dp_size, fsdp_size = lax.axis_size("dp"), lax.axis_size("fsdp")
    layer, place = lax.axis_index("dp"), lax.axis_index("fsdp")
    chips = fsdp_size // 2
    rows = width // (dp_size * fsdp_size)
    position = jnp.arange(width, dtype=jnp.int32)
    row = position % rows
    layer_of = (position // rows) % dp_size ^ layer
    chip_of = (position // (rows * dp_size)) % chips ^ (place // 2)
    core_of = position // (rows * dp_size * chips) ^ (place % 2)
    source = ((layer_of * chips + chip_of) * 2 + core_of) * rows + row
    return (position[:, None] == source[None, :]).astype(BF16)


def local(
    tokens_in, w_qkv, w_attn_out, gain_attn, gain_ffn, rel_bias, router, w_in, w_out,
    segment_ids, expert_ids, d_out,
):
    tok_rows, width = tokens_in.shape
    top_count = expert_ids.shape[1]
    fsdp_size = lax.axis_size("fsdp")
    experts = fsdp_size // 2
    slots = min(tok_rows, tok_rows * top_count * 5 // (4 * experts))
    me = lax.axis_index("fsdp") // 2

    own_in = lax.all_gather(w_in, "dp", axis=0, tiled=True)
    own_out = lax.all_gather(w_out, "dp", axis=0, tiled=True)
    small = jnp.concatenate(
        [router, gain_attn[:, None], gain_ffn[:, None], rel_bias[:, None]], axis=1
    )
    small = jnp.pad(small, ((0, 0), (0, 128 - small.shape[1])))
    relative = expert_ids ^ me
    hot = jnp.sum(
        (relative[:, :, None] == jnp.arange(experts, dtype=jnp.int32)).astype(jnp.int32), axis=1
    )
    rank = jnp.cumsum(hot, axis=0) - hot
    dest = jnp.where(hot > 0, rank, -1)
    lines = max(8, experts)
    dest_row = jnp.pad(dest.T, ((0, lines - experts), (0, 0)), constant_values=-1)

    def exchange(pieces):
        return [pieces[0]] + [
            lax.ppermute(pieces[m], "fsdp", pairs_of(fsdp_size, 2 * m)) for m in range(1, experts)
        ]

    line = gather_line(jnp.concatenate([w_qkv, w_attn_out, small], axis=1))
    sent_grads = dispatch(
        experts, dest_row, d_out, jnp.zeros((lines, tok_rows), F32), slots, (line,)
    )
    move = position_matrix(width)
    (tokens_after,) = held([tokens_in], (line,))
    tokens = tokens_after.astype(F32)
    scale = lax.rsqrt(jnp.mean(tokens * tokens, axis=1, keepdims=True) + EPS)
    unit = jnp.dot(tokens_after, move, preferred_element_type=F32) * scale
    plane, plane_rest, full = gather_plane(line, (sent_grads[1], unit))
    grads_in = exchange([sent_grads[0]] + list(held(sent_grads[1:], (plane,))))

    moved_gain = full[:, 4 * width + experts].astype(F32).reshape(1, width)
    columns = jnp.dot(move, full[:, 4 * width :], preferred_element_type=F32).astype(BF16)
    back_qkv = jnp.dot(move, full[:, : 3 * width], preferred_element_type=F32).astype(BF16)
    back_attn = jnp.dot(
        move, full[:, 3 * width : 4 * width], preferred_element_type=F32
    ).astype(BF16)
    by_row = columns.T
    gain_a = by_row[experts : experts + 1].astype(F32)
    gain_f = by_row[experts + 1 : experts + 2].astype(F32)
    table = by_row[experts + 2].reshape(HEADS, BUCKETS)
    bucket_hot = (
        buckets_of(jnp.arange(BLK, dtype=jnp.int32))[:, None]
        == jnp.arange(BUCKETS, dtype=jnp.int32)[None, :]
    )
    near = jnp.dot(table, bucket_hot.T.astype(BF16), preferred_element_type=F32)
    near = near.reshape(HEADS // 2, 2, BLK)
    far = table[:, BUCKETS - 1].astype(F32)
    place = jnp.arange(128, dtype=jnp.int32)
    swap = ((place[:, None] ^ me) == place[None, :]) & (place[:, None] < experts)
    router_cols = jnp.dot(columns, swap.astype(BF16), preferred_element_type=F32).astype(BF16)
    router_rows = router_cols.T[: max(8, experts)].astype(F32)

    normed_attn = (unit * moved_gain).astype(BF16)
    qkv_rows = jnp.dot(normed_attn, full[:, : 3 * width], preferred_element_type=F32).astype(BF16)
    segments = segment_ids.reshape(tok_rows)
    mixed, lse = attention_forward(qkv_rows, segments, near, far, HEADS)
    residual, normed_ffn, gates, gate_row, moved_mixed = post_attention(
        mixed, plane, plane_rest, tokens_in, gain_f, router_cols, dest_row, move,
    )
    (own_in,) = held([own_in], (plane,))
    other_in = lax.ppermute(own_in, "fsdp", pairs_of(fsdp_size, 1))
    sent_rows = dispatch(experts, dest_row, normed_ffn, gate_row, slots, tuple(grads_in[1:]) + (other_in,))
    rows_in = exchange(sent_rows)
    (own_out,) = held([own_out], (sent_rows[0],))
    other_out = lax.ppermute(own_out, "fsdp", pairs_of(fsdp_size, 1))

    chunks, backs = [], []
    for m in range(experts):
        ahead = tuple(backs[1 : m - 1]) + ((chunks[-1][4],) if chunks else ())
        chunks.append(
            expert_chunk(rows_in[m], grads_in[m], own_in, own_out, other_in, other_out, ahead)
        )
        back = chunks[-1][4]
        backs.append(
            lax.ppermute(back, "fsdp", pairs_of(fsdp_size, 2 * m)) if m > 0 else back
        )
    hid_own, hid_other, dpre_own, dpre_other, _, made, rows_turned, gexp_turned = zip(*chunks)

    def owners(pair):
        return lax.psum_scatter(pair, "dp", scatter_dimension=0, tiled=True)

    swapped = pairs_of(fsdp_size, 1)
    normed_turned, mixed_turned = normed_attn.T, moved_mixed.T
    grad_in_own = weight_grad(rows_turned, dpre_own, tuple(backs[-2:-1]))
    grad_out_own = weight_grad(gexp_turned, hid_own, (grad_in_own,))
    grad_in_other = weight_grad(
        rows_turned, dpre_other, (grad_out_own,) + tuple(backs[-1:])
    )
    grad_out_other = weight_grad(gexp_turned, hid_other, (grad_in_other,))
    got_in = lax.ppermute(grad_in_other, "fsdp", swapped)
    (grad_out_other,) = held([grad_out_other], (got_in,))
    got_out = lax.ppermute(grad_out_other, "fsdp", swapped)
    pair_in = (grad_in_own.astype(F32) + got_in.astype(F32)).astype(BF16)
    (got_out,) = held(
        [got_out], (pair_in, back_attn, normed_turned, mixed_turned, router_rows)
    )
    pair_out = (grad_out_own.astype(F32) + got_out.astype(F32)).astype(BF16)
    middle = pair_out.shape[1] // 2
    d_w_in = owners(pair_in)
    d_w_out = [owners(pair_out[:, :middle]), owners(pair_out[:, middle:])]
    mades = exchange([made[0]] + list(held(made[1:], (pair_out,))))

    d_residual, d_branch, d_mixed, d_gain_f, d_logits = combine_back(
        backs, dest_row, gates, residual, d_out, gain_f, router_rows, back_attn,
        (pair_out,),
    )
    d_qkv, near_grad, far_grad = attention_backward(
        qkv_rows, d_mixed, mixed, lse, segments, near, far, HEADS
    )
    near_grad, far_grad = held([near_grad, far_grad], tuple(mades[1:]))
    d_router = jnp.dot(normed_ffn.T, d_logits.astype(BF16), preferred_element_type=F32)
    d_router = jnp.dot(d_router, swap.T.astype(F32), precision=lax.Precision.HIGHEST)
    d_table = jnp.dot(
        near_grad.reshape(HEADS, BLK), bucket_hot.astype(F32), precision=lax.Precision.HIGHEST
    )
    last = jnp.arange(BUCKETS, dtype=jnp.int32)[None, :] == BUCKETS - 1
    d_table = d_table + jnp.where(last, far_grad[:, :, :1].reshape(HEADS, 1), 0.0)
    late_cols = jnp.where(place[None, :] == experts, d_gain_f.reshape(width, 1), d_router)
    late_cols = jnp.where(place[None, :] == experts + 1, d_table.reshape(width, 1), late_cols)
    late_cols = jnp.dot(move.T, late_cols.astype(BF16), preferred_element_type=F32)
    late_cols = late_cols.astype(BF16)
    keep, send = qkv_grad(
        normed_turned, d_qkv, mixed_turned, d_branch, late_cols, (d_w_in,)
    )
    keep, send = held([keep, send], (d_w_out[0],))
    late = scatter_plane(scatter_pair(keep, send))
    block_out = combine_output(mades, dest_row, gates, residual)
    d_tokens = final_tokens(d_qkv, back_qkv, tokens_in, gain_a, d_residual, (block_out,))
    (late,) = held([late], (d_tokens, d_w_out[1]))
    late = scatter_line(late)
    own_qkv = late[:, : 3 * width]
    own_gain_a = jnp.sum(own_qkv * w_qkv.astype(F32), axis=1) / gain_attn.astype(F32)
    return (
        block_out,
        d_tokens,
        own_qkv,
        late[:, 3 * width : 4 * width],
        own_gain_a,
        late[:, 4 * width + experts],
        late[:, 4 * width + experts + 1],
        late[:, 4 * width : 4 * width + experts],
        d_w_in.astype(F32),
        jnp.concatenate(d_w_out, axis=1).astype(F32),
    )


def solution(mesh):
    both = P(("dp", "fsdp"), None)
    line = P(("dp", "fsdp"))
    tiles = P("dp", "fsdp")
    return jax.shard_map(
        local,
        mesh=mesh,
        in_specs=(both, both, both, line, line, line, both, tiles, tiles, both, both, both),
        out_specs=(both, both, both, both, line, line, line, both, tiles, tiles),
        check_vma=False,
    )
```
